128 devices in a mesh: tm: 8 (over y, core), space: 16 (over z, x).
Axes of the slice: x: 4, y: 4, z: 4, core: 2. Of those that a mesh axis runs over, the one named last changes fastest.
Arguments:
- vorticity: float32 [512, 8192], P('space'), may hold values from -6 to 6
- stream: float32 [512, 8192], P('space'), may hold values from -0.8 to 0.8
- forcing: float32 [512, 8192], P('space'), may hold values from -1.2 to 1.2, as said below
- conv_in: float32 [8, 3, 3], replicated, may hold values from -2 to 2
- conv_out: float32 [8, 3, 3], replicated, may hold values from -0.75 to 0.75
Outputs:
- slice_ends: float32 [8, 512, 8192], P('tm', 'space')
The draws below stay inside these ranges and needn't reach their ends.
Inputs may be any that keep to these rules, and one draw needn't show every extreme that they name: `forcing`: a vorticity source field.
All inputs are finite; a program needn't handle non-finite values.
Results may differ from the reference program's by a relative error of at most 0.0001.
Values sent between devices are 32-bit elements; how exact they have to be, the bound alone decides.
A program may use at most 128 MiB of HBM per device.

```python
import jax
import jax.numpy as jnp

NX = 8192
CH = 8
STEPS = 4
ITERS = 2
NY = 512
SLICES = 8


def draw_forcing(key, part):
    key = jax.random.fold_in(key, 11)
    return 0.3 * jnp.clip(jax.random.normal(key, (NY, NX), jnp.float32), -4.0, 4.0)


def levels(own_key, extent, shards, low, top_value):
    factor_of = 1.0
    for axis_at, shards_of in shards:
        steps = jax.random.uniform(jax.random.fold_in(jax.random.fold_in(own_key, 6), axis_at), (shards_of,), jnp.float32, low / len(shards), top_value / len(shards))
        factor_of = factor_of * jnp.repeat(jnp.exp(steps), extent[axis_at] // shards_of).reshape((-1,) + (1,) * (len(extent) - 1 - axis_at))
    return factor_of


def gaussian(stream_key, extent, scale, limit, cuts=(), held_as=jnp.bfloat16):
    level = levels(stream_key, extent, cuts, -0.22, 0.18) if cuts else 1.0
    drawn = jax.random.normal(stream_key, extent, jnp.float32) * scale * level
    return jnp.minimum(jnp.maximum(drawn, -limit), limit).astype(held_as)


def setup_inputs(seed: int = 0) -> dict:
    key_list = jax.random.split(jax.random.key(seed), 6)
    vorticity = gaussian(key_list[0], (NY, NX), 1.0, 6.0, ((0, 16),), jnp.float32)
    stream = gaussian(key_list[1], (NY, NX), 0.2, 0.8, ((0, 16),), jnp.float32)
    forcing = draw_forcing(jax.random.fold_in(key_list[5], 71), 0)
    conv_in = gaussian(key_list[3], (CH, 3, 3), 9 ** -0.5, 2.0, (), jnp.float32)
    conv_out = gaussian(key_list[4], (CH, 3, 3), (9 * CH) ** -0.5, 0.75, (), jnp.float32)
    return {"vorticity": vorticity, "stream": stream, "forcing": forcing, "conv_in": conv_in, "conv_out": conv_out}


time_step = 1.0
viscosity = 0.1
drag_rate = 0.05
coarse_gain = 0.5


def wrap_rows(values, width):
    return jnp.concatenate([values[..., -width:, :], values, values[..., :width, :]], axis=-2)


def field_rhs(padded, vel_x, vel_y, source):
    centre = padded[..., 1:-1, :]
    right = jnp.roll(centre, -1, axis=-1)
    left = jnp.roll(centre, 1, axis=-1)
    above = padded[..., 2:, :]
    below = padded[..., :-2, :]
    grad_x = (right - left) * 0.5
    grad_y = (above - below) * 0.5
    laplace = above + below + right + left - 4.0 * centre
    return -(vel_x * grad_x + vel_y * grad_y) + viscosity * laplace - drag_rate * centre + source


def velocities(stream_ext):
    centre = stream_ext[1:-1]
    vel_x = (stream_ext[2:] - stream_ext[:-2]) * 0.5
    vel_y = -(jnp.roll(centre, -1, axis=-1) - jnp.roll(centre, 1, axis=-1)) * 0.5
    return vel_x, vel_y


def restrict(values):
    lead = values.shape[:-2]
    row_count, col_count = values.shape[-2], values.shape[-1]
    blocks = values.reshape(lead + (row_count // 4, 4, col_count // 4, 4))
    return jnp.mean(blocks, axis=(-3, -1))


def prolong(coarse):
    return jnp.repeat(jnp.repeat(coarse, 4, axis=-2), 4, axis=-1)


def spread(padded, conv_in):
    row_count = padded.shape[0] - 2
    summed = jnp.zeros((conv_in.shape[0], row_count, padded.shape[1]), jnp.float32)
    for row_shift in range(3):
        for col_shift in range(3):
            moved = jnp.roll(padded[row_shift:row_shift + row_count], 1 - col_shift, axis=-1)
            summed = summed + conv_in[:, row_shift, col_shift][:, None, None] * moved[None]
    return summed


def collect(hidden, conv_out):
    row_count = hidden.shape[1] - 2
    summed = jnp.zeros((row_count, hidden.shape[2]), jnp.float32)
    for row_shift in range(3):
        for col_shift in range(3):
            moved = jnp.roll(hidden[:, row_shift:row_shift + row_count], 1 - col_shift, axis=-1)
            summed = summed + jnp.sum(conv_out[:, row_shift, col_shift][:, None, None] * moved, axis=0)
    return summed


def coarse_advance(padded, conv_in, conv_out):
    hidden = jnp.tanh(spread(padded, conv_in))
    return padded[2:-2] + coarse_gain * collect(hidden, conv_out)


def reference(vorticity, stream, forcing, conv_in, conv_out):
    vel_x, vel_y = velocities(wrap_rows(stream, 1))
    first_coarse = restrict(vorticity)

    def run_chain(corrections):
        coarse = first_coarse
        states = []
        advanced_all = []
        for position in range(SLICES):
            states.append(coarse)
            advanced = coarse_advance(wrap_rows(coarse, 2), conv_in, conv_out)
            advanced_all.append(advanced)
            coarse = advanced + corrections[position]
        return jnp.stack(states), jnp.stack(advanced_all)

    def slope(state):
        return field_rhs(wrap_rows(state, 1), vel_x, vel_y, forcing)

    def fine_run(state):
        for counter in range(STEPS):
            slope_one = slope(state)
            slope_two = slope(state + (0.5 * time_step) * slope_one)
            slope_three = slope(state + (0.5 * time_step) * slope_two)
            slope_four = slope(state + time_step * slope_three)
            state = state + (time_step / 6.0) * (slope_one + 2.0 * slope_two + 2.0 * slope_three + slope_four)
        return state

    zero_terms = jnp.zeros((SLICES,) + first_coarse.shape, jnp.float32)
    states, g_old = run_chain(zero_terms)
    starts = jnp.concatenate([vorticity[None], prolong(states[1:])], axis=0)
    slice_ends = starts
    for iteration in range(ITERS):
        fine = fine_run(starts)
        corrections = restrict(fine) - g_old
        states, g_new = run_chain(corrections)
        slice_ends = fine + prolong(g_new - g_old)
        starts = jnp.concatenate([vorticity[None], slice_ends[:-1]], axis=0)
        g_old = g_new
    return slice_ends
```

```python
import functools

import jax
import jax.numpy as jnp
from jax import lax
from jax.experimental import pallas as pl
from jax.experimental.pallas import tpu as pltpu
from jax.sharding import PartitionSpec as P

STEPS = 4
HALO = 4 * STEPS
LANES = 128
VMEM = pltpu.VMEM
HIGH = lax.Precision.HIGHEST
BIG = 60 * 2**20


def lane_iota():
    return lax.broadcasted_iota(jnp.int32, (8, LANES), 1)


def shifted_tiles(tiles, up):
    count = len(tiles)
    lane = lane_iota()
    rolled = [pltpu.roll(t, LANES - 1 if up else 1, 1) for t in tiles]
    if up:
        return [jnp.where(lane == LANES - 1, rolled[(i + 1) % count], rolled[i]) for i in range(count)]
    return [jnp.where(lane == 0, rolled[i - 1], rolled[i]) for i in range(count)]


def coarse_step(n, w_in, w_out, extra, win, gbuf, taps, sums, parts):
    lanes, rows = win.shape[0], win.shape[1]
    count = -(-(rows - 4 * n) // 8)
    off = min(2 * n, rows // 2 - 4 * count)
    at = [pl.ds(off + q, 8, stride=count) for q in range(count)]
    for q in range(count):
        x = [win[l, at[q], :] for l in range(lanes)]
        down, up = shifted_tiles(x, False), shifted_tiles(x, True)
        for l in range(lanes):
            for d, v in enumerate((down[l], x[l], up[l])):
                taps[d, l, q + 1] = v
                if q == 0:
                    taps[d, l, count + 1] = pltpu.roll(v, 7, 0)
                if q == count - 1:
                    taps[d, l, 0] = pltpu.roll(v, 1, 0)

    def tile(l, _):
        for q0 in range(0, count, 2):
            qs = range(q0, min(q0 + 2, count))
            acc = {q: [None] * 9 for q in qs}
            for h in range(8):
                pre = {q: None for q in qs}
                for k in range(9):
                    w = w_in[h * 9 + k]
                    for q in qs:
                        v = w * taps[k % 3, l, q + k // 3]
                        pre[q] = v if pre[q] is None else pre[q] + v
                hid = {q: jnp.tanh(pre[q]) for q in qs}
                for k in range(9):
                    w = w_out[h * 9 + k]
                    for q in qs:
                        v = w * hid[q]
                        acc[q][k] = v if acc[q][k] is None else acc[q][k] + v
            for q in qs:
                for k in range(9):
                    sums[k, l, q] = acc[q][k]
        return 0

    lax.fori_loop(0, lanes, tile, 0)
    for q in range(count):
        for dy in range(3):
            low = shifted_tiles([sums[dy * 3, l, q] for l in range(lanes)], False)
            high = shifted_tiles([sums[dy * 3 + 2, l, q] for l in range(lanes)], True)
            for l in range(lanes):
                v = low[l] + high[l] + sums[dy * 3 + 1, l, q]
                parts[dy, l, q + 1] = v
                if q == 0 and dy == 2:
                    parts[dy, l, count + 1] = pltpu.roll(v, 7, 0)
                if q == count - 1 and dy == 0:
                    parts[dy, l, 0] = pltpu.roll(v, 1, 0)
    for q in range(count):
        for l in range(lanes):
            g = taps[1, l, q + 1] + (parts[0, l, q] + parts[1, l, q + 1] + parts[2, l, q + 2])
            gbuf[l, at[q], :] = g
            if extra is not None:
                win[l, at[q], :] = g + extra(l, at[q])


def coarse_scratch(lanes, rows):
    most = rows // 8
    return [
        VMEM((lanes, rows, LANES), jnp.float32),
        VMEM((lanes, rows, LANES), jnp.float32),
        VMEM((3, lanes, most + 2, 8, LANES), jnp.float32),
        VMEM((9, lanes, most, 8, LANES), jnp.float32),
        VMEM((3, lanes, most + 2, 8, LANES), jnp.float32),
        VMEM((72, 8, LANES), jnp.float32),
        VMEM((72, 8, LANES), jnp.float32),
    ]


def fill_weights(conv_in, conv_out, w_in, w_out):
    for k in range(72):
        w_in[k] = jnp.full((8, LANES), conv_in[k], jnp.float32)
        w_out[k] = jnp.full((8, LANES), 0.5 * conv_out[k], jnp.float32)


def coarse_kernel(conv_in, conv_out, start_ref, extra_ref, g_ref, win, gbuf, taps, sums, parts, w_in, w_out):
    lanes, rows = win.shape[0], win.shape[1]
    slices = g_ref.shape[0]
    centre = (rows - 8) // 2
    fill_weights(conv_in, conv_out, w_in, w_out)
    win[...] = start_ref[...]
    for n in range(slices):
        extra = None if n + 1 == slices else lambda l, at, n=n: extra_ref[n, l, at, :]
        coarse_step(n, w_in, w_out, extra, win, gbuf, taps, sums, parts)
        for l in range(lanes):
            g_ref[n, l] = gbuf[l, centre : centre + 8, :]


def coarse_chain(conv_in, conv_out, start, extra):
    slices, lanes, rows = extra.shape[:3]
    smem = pl.BlockSpec(memory_space=pltpu.SMEM)
    vmem = pl.BlockSpec(memory_space=VMEM)
    return pl.pallas_call(
        coarse_kernel,
        name="coarse_chain",
        out_shape=jax.ShapeDtypeStruct((slices, lanes, 8, LANES), jnp.float32),
        in_specs=[smem, smem, vmem, vmem],
        out_specs=vmem,
        scratch_shapes=coarse_scratch(lanes, rows),
        compiler_params=pltpu.CompilerParams(vmem_limit_bytes=BIG),
    )(conv_in.reshape(72), conv_out.reshape(72), start, extra)


def fine_stage(src, base, dst, pcoef, qcoef, force, off, count, alpha):
    tiles = src.shape[0]
    group = 2 if count > 6 else 4
    at = [pl.ds(off + q, 8, stride=count) for q in range(count)]
    beta = 0.2 * alpha

    def body(g, _):
        lane = lane_iota()
        first, last = lane == 0, lane == LANES - 1
        c = [lax.rem(g * group + (k - 1) + tiles, tiles) for k in range(group + 2)]
        x = [[src[c[k], at[q], :] for q in range(count)] for k in range(group + 2)]
        right = [None if k == 0 else [pltpu.roll(v, LANES - 1, 1) for v in x[k]] for k in range(group + 2)]
        left = [None if k == group + 1 else [pltpu.roll(v, 1, 1) for v in x[k]] for k in range(group + 2)]
        for k in range(1, group + 1):
            above = x[k][1:] + [pltpu.roll(x[k][0], 7, 0)]
            below = [pltpu.roll(x[k][-1], 1, 0)] + x[k][:-1]
            for q in range(count):
                r = jnp.where(last, right[k + 1][q], right[k][q])
                l = jnp.where(first, left[k - 1][q], left[k][q])
                slot = (c[k], at[q], slice(None))
                t = pcoef[slot] * (r - l) + qcoef[slot] * (above[q] - below[q])
                t = t + (l + below[q]) + (force[slot] - 2.25 * x[k][q])
                dst[slot] = base[slot] + beta * t
        return 0

    lax.fori_loop(0, tiles // group, body, 0)


def fine_kernel(
    use_ref, top, mid, bottom, coarse, s_top, s_mid, s_bottom, f_top, f_mid, f_bottom,
    out, mean, state, one, two, pcoef, qcoef, force, narrow, wide, packed,
):
    tiles, rows = state.shape[0], state.shape[1]
    inner = rows - 2 * HALO
    use = use_ref[0] > 0

    def stage_in(c, _):
        lanes = pl.ds(pl.multiple_of(c * LANES, LANES), LANES)
        for ref, rows_at in ((top, slice(0, HALO)), (mid, slice(HALO, HALO + inner)), (bottom, slice(HALO + inner, rows))):
            v = ref[:, lanes]
            state[c, rows_at, :] = jnp.where(use, v, jnp.zeros_like(v))
        for dst, scale, refs in ((one, 1.0, (s_top, s_mid, s_bottom)), (force, 5.0, (f_top, f_mid, f_bottom))):
            for ref, rows_at in zip(refs, (slice(0, HALO), slice(HALO, HALO + inner), slice(HALO + inner, rows))):
                v = ref[:, lanes]
                dst[c, rows_at, :] = v if scale == 1.0 else scale * v
        return 0

    lax.fori_loop(0, tiles, stage_in, 0)
    count = rows // 8
    at = [pl.ds(q, 8, stride=count) for q in range(count)]

    def coefficients(c, _):
        lane = lane_iota()
        before, after = lax.rem(c + tiles - 1, tiles), lax.rem(c + 1, tiles)
        x = [one[c, at[q], :] for q in range(count)]
        for q in range(count):
            above = x[q + 1] if q + 1 < count else pltpu.roll(x[0], 7, 0)
            below = x[q - 1] if q else pltpu.roll(x[count - 1], 1, 0)
            pcoef[c, at[q], :] = 0.5 - 1.25 * (above - below)
            r = jnp.where(lane == LANES - 1, pltpu.roll(one[after, at[q], :], LANES - 1, 1), pltpu.roll(x[q], LANES - 1, 1))
            l = jnp.where(lane == 0, pltpu.roll(one[before, at[q], :], 1, 1), pltpu.roll(x[q], 1, 1))
            qcoef[c, at[q], :] = 0.5 + 1.25 * (r - l)
        return 0

    lax.fori_loop(0, tiles, coefficients, 0)

    blocks = tiles // 4
    copies = jnp.where(
        lax.broadcasted_iota(jnp.int32, (LANES, 4 * LANES), 0)
        == lax.broadcasted_iota(jnp.int32, (LANES, 4 * LANES), 1) // 4,
        1.0, 0.0,
    ).astype(jnp.float32)
    for m in range(blocks):
        narrow[m] = coarse[:, m * LANES : (m + 1) * LANES]
    for half in range(2):
        compact = jnp.concatenate([narrow[m, pl.ds(half, 8, stride=2), :] for m in range(blocks)], axis=0)
        wide[half] = jnp.dot(compact, copies, precision=HIGH, preferred_element_type=jnp.float32)

    def add_coarse(m, _):
        for half in range(2):
            for k in range(4):
                v = wide[half, pl.ds(pl.multiple_of(m * 8, 8), 8), k * LANES : (k + 1) * LANES]
                for q in range(4):
                    slot = (m * 4 + k, at[half * 4 + q], slice(None))
                    state[slot] = state[slot] + v
        return 0

    lax.fori_loop(0, blocks, add_coarse, 0)

    for step in range(STEPS):
        off = 4 * step
        count = (rows - 2 * off) // 8
        shared = (pcoef, qcoef, force, off, count)
        fine_stage(state, state, one, *shared, 0.25)
        fine_stage(one, state, two, *shared, 1.0 / 3.0)
        fine_stage(two, state, one, *shared, 0.5)
        fine_stage(one, state, state, *shared, 1.0)

    def stage_out(m, _):
        for k in range(4):
            c = m * 4 + k
            lanes = pl.ds(pl.multiple_of(c * LANES, LANES), LANES)
            out[:, lanes] = state[c, HALO : HALO + inner, :]
            four = [state[c, pl.ds(HALO + q, 8, stride=4), :] for q in range(4)]
            packed[pl.ds(pl.multiple_of(m * 8, 8), 8), k * LANES : (k + 1) * LANES] = (four[0] + four[1]) + (four[2] + four[3])
        return 0

    lax.fori_loop(0, blocks, stage_out, 0)
    averages = jnp.where(
        lax.broadcasted_iota(jnp.int32, (4 * LANES, LANES), 0) // 4
        == lax.broadcasted_iota(jnp.int32, (4 * LANES, LANES), 1),
        0.0625, 0.0,
    ).astype(jnp.float32)
    compact = jnp.dot(packed[...], averages, precision=HIGH, preferred_element_type=jnp.float32)
    for m in range(blocks):
        mean[:, m * LANES : (m + 1) * LANES] = compact[m * 8 : (m + 1) * 8]


def fine(use, base, coarse, stream, forcing):
    inner, cols = base[1].shape
    rows, tiles = inner + 2 * HALO, cols // LANES
    vmem = pl.BlockSpec(memory_space=VMEM)
    whole = VMEM((tiles, rows, LANES), jnp.float32)
    return pl.pallas_call(
        fine_kernel,
        name="fine_propagator",
        out_shape=(
            jax.ShapeDtypeStruct((inner, cols), jnp.float32),
            jax.ShapeDtypeStruct((inner // 4, cols // 4), jnp.float32),
        ),
        in_specs=[pl.BlockSpec(memory_space=pltpu.SMEM)] + [vmem] * 10,
        out_specs=(vmem, vmem),
        scratch_shapes=[whole] * 6
        + [
            VMEM((tiles // 4, rows // 4, LANES), jnp.float32),
            VMEM((2, tiles * 2, 4 * LANES), jnp.float32),
            VMEM((tiles * 2, 4 * LANES), jnp.float32),
        ],
        compiler_params=pltpu.CompilerParams(vmem_limit_bytes=BIG),
    )(use, *base, coarse, *stream, *forcing)


def edges(value, width):
    size = lax.axis_size("space")
    up = [(i, (i + 1) % size) for i in range(size)]
    down = [(j, i) for i, j in up]
    before = lax.ppermute(value[..., -width:, :], "space", up)
    after = lax.ppermute(value[..., :width, :], "space", down)
    return before, after


def restrict(values):
    row_count, col_count = values.shape
    return jnp.mean(values.reshape((row_count // 4, 4, col_count // 4, 4)), axis=(1, 3))


def prolong(coarse):
    return jnp.repeat(jnp.repeat(coarse, 4, axis=-2), 4, axis=-1)


def body(vorticity, stream, forcing, conv_in, conv_out):
    t = lax.axis_index("tm")
    slices = lax.axis_size("tm")
    cols = vorticity.shape[1] // 4
    own = cols // slices
    lanes = own // LANES + 1
    half = LANES // 2

    def windows(v):
        wide = jnp.concatenate([v[..., -half:], v, v[..., :half]], axis=-1)
        return jnp.stack([wide[..., i * own : (i + 1) * own + LANES] for i in range(slices)])

    def tall(v):
        one_up, one_down = edges(v, 8)
        both = edges(jnp.concatenate([one_up, one_down], axis=-2), 16)
        two_up, two_down = both[0][..., :8, :], both[1][..., 8:, :]
        return jnp.concatenate([two_up, one_up, v, one_down, two_down], axis=-2)

    def tiled(v):
        return jnp.swapaxes(v.reshape(v.shape[:-1] + (lanes, LANES)), -2, -3)

    def centre(g):
        g = jnp.swapaxes(g, -2, -3).reshape(slices, 8, lanes * LANES)
        return g[..., half:-half]

    def exchange(v):
        return lax.all_to_all(v, "tm", 0, 0)

    def to_slices(parts):
        got = exchange(jnp.stack(parts, axis=1))
        return jnp.moveaxis(got, 0, 2).reshape(len(parts), 8, cols)

    first = restrict(vorticity)
    wide = jnp.concatenate([first[:, -half:], first, first[:, :half]], axis=1)
    start = tiled(tall(lax.dynamic_slice_in_dim(wide, t * own, own + LANES, axis=1)))

    stream_edges = edges(stream, HALO)
    forcing_edges = edges(forcing, HALO)
    vort_edges = edges(vorticity, HALO)
    streams = (stream_edges[0], stream, stream_edges[1])
    forcings = (forcing_edges[0], forcing, forcing_edges[1])
    vorts = (vort_edges[0], vorticity, vort_edges[1])

    zero = jnp.zeros((slices,) + start.shape, jnp.float32)
    g1 = centre(coarse_chain(conv_in, conv_out, start, zero))
    before = jnp.concatenate([g1[:1], g1[:1], g1[:-2]])
    last = jnp.concatenate([g1[:1], g1[:-1]])
    got = to_slices([before, last])
    state_c, g_old = got[0], got[1]
    near = edges(state_c, 4)
    coarse16 = jnp.concatenate([near[0], state_c, near[1]], axis=0)
    early = t <= 1
    coarse16 = jnp.where(early, 0.0, coarse16)
    use = early.astype(jnp.int32).reshape(1)
    fine1, mean1 = fine(use, vorts, coarse16, streams, forcings)

    fine_edges = edges(fine1, HALO)
    corr = tall(exchange(windows(mean1 - g_old)))
    corr = jnp.concatenate([corr[1:], jnp.zeros_like(corr[:1])])
    g2 = centre(coarse_chain(conv_in, conv_out, start, tiled(corr)))
    change = g2 - g1
    change = jnp.concatenate([jnp.zeros_like(change[:1]), change[:-1]])
    got = to_slices([change, g2])
    delta, g_old = got[0], got[1]
    near = edges(delta, 4)
    coarse16 = jnp.concatenate([near[0], delta, near[1]], axis=0)
    fine2, mean2 = fine(
        jnp.ones((1,), jnp.int32), (fine_edges[0], fine1, fine_edges[1]), coarse16, streams, forcings
    )
    fine2 = jnp.where(t == 0, fine1, fine2)
    mean2 = jnp.where(t == 0, mean1, mean2)

    corr = tall(exchange(windows(mean2 - g_old)))
    g3 = centre(coarse_chain(conv_in, conv_out, start, tiled(corr)))
    delta = to_slices([g3 - g2])[0]
    return (fine2 + prolong(delta))[None]


def solution(mesh):
    placed = (P("space", None), P("space", None), P("space", None), P(), P())
    return jax.shard_map(
        body, mesh=mesh, in_specs=placed, out_specs=P("tm", "space", None), check_vma=False
    )
```

```python
import functools
import math

import jax
import jax.numpy as jnp
import numpy as np
from jax import lax
from jax.experimental import pallas as pl
from jax.experimental.pallas import tpu as pltpu
from jax.sharding import PartitionSpec as P

F32 = jnp.float32
VMEM = pltpu.VMEM
MESH = pl.DeviceIdType.MESH
HIGH = lax.Precision.HIGHEST

STEPS = 4
SLICES = 8
LANES = 128
CHUNK = 64
INNER = 32
HALO = 16
PAD = 8
TALL = INNER + 2 * HALO + 2 * PAD
OWN = PAD + HALO
PITCH = 33
BLOCKS = 16
REACH = 28
WINDOW = 2 * REACH


def fine_weights():
    shift = np.polynomial.Polynomial([-0.45, 0.2])
    of_w = sum(shift**j / math.factorial(j) for j in range(5))
    of_f = sum(shift**j / math.factorial(j + 1) for j in range(4))
    return [float(v) for v in of_w.coef], [float(v) for v in of_f.coef] + [0.0]


def lane_iota():
    return lax.broadcasted_iota(jnp.int32, (8, LANES), 1)


def lane_shifted(value, up):
    lane = lax.broadcasted_iota(jnp.int32, value.shape, 2)
    if up:
        rolled = pltpu.roll(value, LANES - 1, 2)
        return jnp.where(lane == LANES - 1, jnp.concatenate([rolled[1:], rolled[:1]], axis=0), rolled)
    rolled = pltpu.roll(value, 1, 2)
    return jnp.where(lane == 0, jnp.concatenate([rolled[-1:], rolled[:-1]], axis=0), rolled)


def lane_gather(value, index):
    return jnp.take_along_axis(value, index, axis=1)


def next_chunk():
    lane = lane_iota()
    return jnp.where(lane < 64, lane + 64, jnp.where(lane == 127, 0, lane - 63))


def previous_chunk():
    lane = lane_iota()
    return jnp.where(lane >= 64, lane - 64, jnp.where(lane == 0, 127, lane + 63))


def swap_tiles_and_lanes(tiles):
    lane = lane_iota()
    for bit in range(4):
        width = 4 << bit
        high = (lane // width) % 2 == 1
        out = list(tiles)
        for m in range(16):
            if not m >> bit & 1:
                a, b = tiles[m], tiles[m | 1 << bit]
                out[m] = jnp.where(high, pltpu.roll(b, width, 1), a)
                out[m | 1 << bit] = jnp.where(high, b, pltpu.roll(a, LANES - width, 1))
        tiles = out
    return tiles


def to_chunks(tiles):
    lane = lane_iota()
    index = ((lane % 4) * 2 + lane // 64) * 16 + (lane % 64) // 4
    return swap_tiles_and_lanes([lane_gather(t, index) for t in tiles])


def from_chunks(tiles):
    lane = lane_iota()
    block = lane // 16
    index = (block % 2) * 64 + (lane % 16) * 4 + block // 2
    return [lane_gather(t, index) for t in swap_tiles_and_lanes(tiles)]


def coarse_step(count, w_in, w_out, win, values, extra, taps, sums, parts):
    lanes = win.shape[0]
    off = REACH - 4 * count
    at = [pl.ds(off + q, 8, stride=count) for q in range(count)]

    def tiles(q):
        return slice(lanes * q, lanes * q + lanes)

    for q in range(count):
        x = win[:, at[q], :]
        for dx, v in enumerate((lane_shifted(x, False), x, lane_shifted(x, True))):
            for dy in range(3):
                place = q + 1 - dy
                if place < 0:
                    taps[dy * 3 + dx, tiles(count - 1)] = pltpu.roll(v, 7, 1)
                elif place >= count:
                    taps[dy * 3 + dx, tiles(0)] = pltpu.roll(v, 1, 1)
                else:
                    taps[dy * 3 + dx, tiles(place)] = v
    total = lanes * count
    group = GROUP

    def few(i, _):
        some = pl.ds(jnp.minimum(i * group, total - group), group)
        x = taps[:, some]
        acc = None
        for h in range(8):
            hidden = jnp.tanh(jnp.sum(w_in[h][:, None] * x, axis=0))
            term = w_out[h][:, None] * hidden[None]
            acc = term if acc is None else acc + term
        sums[:, some] = acc
        return 0

    lax.fori_loop(0, -(-total // group), few, 0)
    for q in range(count):
        for dy in range(3):
            low = lane_shifted(sums[dy * 3, tiles(q)], False)
            high = lane_shifted(sums[dy * 3 + 2, tiles(q)], True)
            v = low + high + sums[dy * 3 + 1, tiles(q)]
            parts[dy, q + 1] = v
            if q == 0 and dy == 2:
                parts[dy, count + 1] = pltpu.roll(v, 7, 1)
            if q == count - 1 and dy == 0:
                parts[dy, 0] = pltpu.roll(v, 1, 1)
    for q in range(count):
        g = win[:, at[q], :] + (parts[0, q] + parts[1, q + 1] + parts[2, q + 2])
        values[:, at[q], :] = g
        if extra is not None:
            win[:, at[q], :] = g + extra(off + q, count)


def own_columns(value):
    rolled = pltpu.roll(value, 64, 2)
    lane = lax.broadcasted_iota(jnp.int32, (2, 8, LANES), 2)
    return jnp.where(lane < 64, rolled[:2], rolled[1:])


def fine_stage(src, dst, base, pcoef, qcoef, force, off, count, scale, of_base):
    at = [pl.ds(off + q, 8, stride=count) for q in range(-1, count + 1)]

    def block(first, size):
        centre = pl.ds(first, size)
        wide = [src[pl.ds(first - 1, size + 2), a, :] for a in at[1:-1]]
        column = [src[centre, at[0], :]] + [x[1:-1] for x in wide] + [src[centre, at[-1], :]]
        results = []
        for q in range(count):
            slot = (centre, at[q + 1], slice(None))
            left, right = wide[q][:-2], wide[q][2:]
            above, below = column[q + 2], column[q]
            t = pcoef[slot] * (right - left) + qcoef[slot] * (above - below) + (left + below)
            if scale != 1.0:
                t = scale * t
            here = column[q + 1] if src is base else base[slot]
            t = t + (of_base * here + force[slot])
            dst[slot] = t
            results.append(t)
        return results

    last = block(CHUNK - 1, 2)
    first = block(1, 2)
    ahead, back = next_chunk(), previous_chunk()
    for q in range(count):
        dst[0, at[q + 1], :] = lane_gather(last[q][1], back)
        dst[CHUNK + 1, at[q + 1], :] = lane_gather(first[q][0], ahead)
    group = 6 if count > 6 else 10

    def body(g, _):
        block(3 + g * group, group)
        return 0

    lax.fori_loop(0, (CHUNK - 4) // group, body, 0)


def fine_run(state, one, two, pcoef, qcoef, force):
    of_w, _ = fine_weights()
    for step in range(STEPS):
        count = 9 if step == 0 else 8 - step
        off = 4 if step == 0 else PAD + 4 * step
        shared = (state, pcoef, qcoef)
        fine_stage(state, one, *shared, force.at[3], off, count, 1.0, of_w[3] / of_w[4])
        fine_stage(one, two, *shared, force.at[2], off, count, 1.0, of_w[2] / of_w[4])
        fine_stage(two, one, *shared, force.at[1], off, count, 1.0, of_w[1] / of_w[4])
        fine_stage(one, state, *shared, force.at[0], off, count, of_w[4], of_w[0])


def ghosts(ref):
    ahead, back = next_chunk(), previous_chunk()
    for r in range(PAD, TALL - PAD, 8):
        ref[0, r : r + 8, :] = lane_gather(ref[CHUNK, r : r + 8, :], back)
        ref[CHUNK + 1, r : r + 8, :] = lane_gather(ref[1, r : r + 8, :], ahead)


def coefficients(stream, forcing, pcoef, qcoef, force):
    of_w, of_f = fine_weights()
    ghosts(stream)
    count = 9
    at = [pl.ds(4 + q, 8, stride=count) for q in range(-1, count + 1)]

    group = 4

    def body(g, _):
        first = 1 + g * group
        c = pl.ds(first, group)
        wide = [stream[pl.ds(first - 1, group + 2), a, :] for a in at[1:-1]]
        x = [stream[c, at[0], :]] + [v[1:-1] for v in wide] + [stream[c, at[-1], :]]
        for q in range(count):
            a = at[q + 1]
            pcoef[c, a, :] = 0.5 - 1.25 * (x[q + 2] - x[q])
            qcoef[c, a, :] = 0.5 + 1.25 * (wide[q][2:] - wide[q][:-2])
            f = forcing[c, a, :]
            force[0, c, a, :] = of_f[0] * f
            for k in range(1, 4):
                force[k, c, a, :] = (of_f[k] / of_w[4]) * f
        return 0

    lax.fori_loop(0, CHUNK // group, body, 0)


def natural_to_rows(source, nat):
    for c in range(64):
        nat[c * PITCH : c * PITCH + INNER, :] = source[:, c * LANES : (c + 1) * LANES]


def rows_to_chunks(nat, lam):
    low = lax.broadcasted_iota(jnp.int32, (64, LANES), 1) < 64
    for i in range(INNER // 2):
        j = i + INNER // 2
        at_i, at_j = pl.ds(i, 64, stride=PITCH), pl.ds(j, 64, stride=PITCH)
        flipped = jnp.concatenate([nat[at_i, :], nat[at_j, :]], axis=0).T
        top, bottom = flipped[:64], flipped[64:]
        lam[at_i, :] = jnp.where(low, top, pltpu.roll(bottom, 64, 1))
        lam[at_j, :] = jnp.where(low, pltpu.roll(top, 64, 1), bottom)


def chunks_to_rows(lam, nat):
    low = lax.broadcasted_iota(jnp.int32, (64, LANES), 1) < 64
    for i in range(INNER // 2):
        j = i + INNER // 2
        at_i, at_j = pl.ds(i, 64, stride=PITCH), pl.ds(j, 64, stride=PITCH)
        x, y = lam[at_i, :], lam[at_j, :]
        top = jnp.where(low, x, pltpu.roll(y, 64, 1))
        bottom = jnp.where(low, pltpu.roll(x, 64, 1), y)
        flipped = jnp.concatenate([top, bottom], axis=0).T
        nat[at_i, :] = flipped[:64]
        nat[at_j, :] = flipped[64:]


def store_own(lam, ref):
    for c in range(CHUNK):
        ref[1 + c, OWN : OWN + INNER, :] = lam[c * PITCH : c * PITCH + INNER, :]


def load_own(ref, lam):
    for c in range(CHUNK):
        lam[c * PITCH : c * PITCH + INNER, :] = ref[1 + c, OWN : OWN + INNER, :]


def spaced_tiles(tiles, rolled):
    lane = lane_iota()
    turned = [pltpu.roll(t, 64, 1) for t in tiles]
    for k in range(BLOCKS):
        v = jnp.where(lane < 64, turned[k - 1], turned[k])
        rolled[k] = v
        if k < 2:
            rolled[BLOCKS + k] = v


def block_means(state):
    tiles = []
    for m in range(BLOCKS):
        four = [state[1 + 4 * m : 5 + 4 * m, pl.ds(OWN + q, 8, stride=4), :] for q in range(4)]
        tiles.append(0.0625 * jnp.sum((four[0] + four[1]) + (four[2] + four[3]), axis=0))
    return from_chunks(tiles)


def coarse_in_chunks(pieces, coarse):
    for half in range(2):
        at = pl.ds(half, 8, stride=2)
        tiles = to_chunks([pieces[m // 2, m % 2, at, :] for m in range(BLOCKS)])
        for m in range(BLOCKS):
            coarse[m, at, :] = tiles[m]


def spread_coarse(coarse, base, state):
    upper = lax.broadcasted_iota(jnp.int32, (8, LANES), 0) < 4

    def body(m, _):
        c = pl.ds(4 * m, 4)
        for r in range(8):
            v = jnp.where(upper, coarse[m, 2 * r : 2 * r + 1, :], coarse[m, 2 * r + 1 : 2 * r + 2, :])[None]
            old = base(c, r)
            v = jnp.broadcast_to(v, (4, 8, LANES)) if old is None else old + v
            state[pl.ds(4 * m + 1, 4), PAD + 8 * r : PAD + 8 * r + 8, :] = v
        return 0

    lax.fori_loop(0, BLOCKS, body, 0)


SLOTS = 64
GROUP = 2


def kernel(
    conv_in, conv_out, vort_hbm, stream_hbm, force_hbm, out,
    inputs, nat, lam, fields, state, one, two, pcoef, qcoef, force,
    start, win, old, new, taps, sums, parts, w_in, w_out,
    rolled, means, sent, got, edge, coarse, packed,
    in_sem, send_sem, recv_sem,
):
    t, z = lax.axis_index("tm"), lax.axis_index("space")
    slabs = lax.axis_size("space")
    parity = lax.rem(t, 2)
    used = [0]

    def slot_of(k):
        return lax.rem(t + k, SLICES)

    def slab_of(d):
        return lax.rem(z + d + slabs, slabs)

    def remote(src, dst, to):
        n = used[0]
        used[0] += 1
        return pltpu.make_async_remote_copy(
            src_ref=src, dst_ref=dst, send_sem=send_sem.at[n], recv_sem=recv_sem.at[n],
            device_id=to, device_id_type=MESH,
        )

    def start_all(copies):
        for c in copies:
            c.start()

    def recv_all(copies):
        for c in copies:
            c.wait_recv()

    def sent_all(copies):
        for c in copies:
            c.wait_send()

    loads = [
        pltpu.make_async_copy(ref, inputs.at[i], in_sem.at[i])
        for i, ref in enumerate((vort_hbm, stream_hbm, force_hbm))
    ]
    start_all(loads)
    barrier = pltpu.get_barrier_semaphore()
    peers = [(slot_of(k), z) for k in range(1, SLICES)] + [(t, slab_of(d)) for d in (-3, -2, -1, 1, 2, 3)]
    for p in peers:
        pl.semaphore_signal(barrier, inc=1, device_id=p, device_id_type=MESH)
    for h in range(8):
        for k in range(9):
            w_in[h, k] = jnp.full((8, LANES), conv_in[h, k // 3, k % 3], F32)
            w_out[h, k] = jnp.full((8, LANES), 0.5 * conv_out[h, k // 3, k % 3], F32)

    loads[0].wait()
    natural_to_rows(inputs.at[0], nat)
    for c in range(64):
        four = [nat[pl.ds(c * PITCH + q, 8, stride=4), :] for q in range(4)]
        m, k = c // 4, c % 4
        packed[m * 8 : m * 8 + 8, k * LANES : (k + 1) * LANES] = (four[0] + four[1]) + (four[2] + four[3])
    averages = jnp.where(
        lax.broadcasted_iota(jnp.int32, (4 * LANES, LANES), 0) // 4
        == lax.broadcasted_iota(jnp.int32, (4 * LANES, LANES), 1), 0.0625, 0.0,
    ).astype(F32)
    first = jnp.dot(packed[...], averages, precision=HIGH, preferred_element_type=F32)
    spaced_tiles([first[m * 8 : m * 8 + 8] for m in range(BLOCKS)], rolled.at[0])
    mine = pl.ds(2 * t, 3)
    pl.semaphore_wait(barrier, len(peers))
    near = [
        remote(rolled.at[0, mine], start.at[:, REACH - 4 - 8 * d : REACH + 4 - 8 * d, :], (t, slab_of(d)))
        for d in (-1, 1, -2, 2, -3, 3)
    ]
    start_all(near)
    start[:, REACH - 4 : REACH + 4, :] = rolled[0, mine]

    @pl.when(t <= 1)
    def _():
        rows_to_chunks(nat, lam)
        store_own(lam, state)

    for i in (1, 2):
        loads[i].wait()
        natural_to_rows(inputs.at[i], nat)
        rows_to_chunks(nat, lam)
        store_own(lam, fields.at[i - 1])
    inside = slice(1, CHUNK + 1)
    low, high = slice(OWN - HALO, OWN), slice(OWN + INNER, OWN + INNER + HALO)
    first_rows, last_rows = slice(OWN, OWN + HALO), slice(OWN + INNER - HALO, OWN + INNER)
    across = [
        remote(fields.at[parity, inside, last_rows], fields.at[parity, inside, low], (t, slab_of(1))),
        remote(fields.at[parity, inside, first_rows], fields.at[parity, inside, high], (t, slab_of(-1))),
    ]
    sibling = (t + 1 - 2 * parity, z)
    shared = [
        remote(fields.at[parity, inside, rows], fields.at[parity, inside, rows], sibling) for rows in (low, high)
    ]
    early = [
        remote(state.at[inside, last_rows], state.at[inside, low], (t, slab_of(1))),
        remote(state.at[inside, first_rows], state.at[inside, high], (t, slab_of(-1))),
    ]

    @pl.when(t <= 1)
    def _():
        start_all(early)

    start_all(across)

    recv_all(near)
    win[...] = start[...]
    scratch = (taps, sums, parts)

    def keep(phase, n, read, rows):
        for r in range(0, rows, 8):
            sent[phase, n, :, r : r + 8, :] = own_columns(read(REACH - rows // 2 + r))

    def rows_of(ref):
        return lambda r: ref[:, r : r + 8, :]

    def nothing(phase, n):
        sent[phase, n] = jnp.zeros(sent.shape[2:], F32)

    def out_copies(phase, shift, rows):
        return [
            remote(
                sent.at[phase, lax.rem(slot_of(k) + shift, SLICES), :, 0:rows],
                got.at[phase, t, :, 0:rows],
                (slot_of(k), z),
            )
            for k in range(1, SLICES)
        ]

    def keep_own(phase, shift):
        got[phase, t] = sent[phase, lax.rem(t + shift, SLICES)]

    plain = lambda row, count: 0.0
    nothing(0, 0)
    nothing(0, 7)
    for n in range(6):
        coarse_step(-(-(44 - 4 * n) // 8), w_in, w_out, win, old.at[n], plain, *scratch)
        keep(0, n + 1, rows_of(win), 16)
    deliver = out_copies(0, SLICES - 1, 16)
    start_all(deliver)
    keep_own(0, SLICES - 1)
    for n in (6, 7):
        coarse_step(-(-(44 - 4 * n) // 8), w_in, w_out, win, old.at[n], plain if n < 7 else None, *scratch)

    recv_all(across)
    start_all(shared)
    recv_all(shared)
    coefficients(fields.at[0], fields.at[1], pcoef, qcoef, force)
    recv_all(deliver)

    @pl.when(t <= 1)
    def _():
        recv_all(early)
        sent_all(early)

    @pl.when(t > 1)
    def _():
        coarse_in_chunks(got.at[0], coarse)
        spread_coarse(coarse, lambda c, r: None, state)

    ghosts(state)
    fine_run(state, one, two, pcoef, qcoef, force)

    def share_means(phase, shift, plus_one, plus_two):
        spaced_tiles(block_means(state), rolled.at[phase + 1])
        place = lax.rem(t + shift, SLICES)
        middle = slice(16, 24)
        copies = [
            remote(rolled.at[phase + 1, pl.ds(2 * slot_of(k), 3)], means.at[phase, place, :, middle], (slot_of(k), z))
            for k in range(1, SLICES)
        ]
        start_all(copies)
        means[phase, place, :, middle, :] = rolled[phase + 1, pl.ds(2 * t, 3)]
        around = [
            remote(
                means.at[phase, slice(*slots), :, middle],
                means.at[phase, slice(*slots), :, 16 - 8 * d : 24 - 8 * d],
                (t, slab_of(d)),
            )
            for d, slots in ((-1, plus_one), (1, plus_one), (-2, plus_two), (2, plus_two))
        ]
        return copies, around

    to_slots, around = share_means(0, SLICES - 1, (0, 7), (0, 4))
    bulk = [
        [
            remote(state.at[part, last_rows], edge.at[0, keep_part], (t, slab_of(1))),
            remote(state.at[part, first_rows], edge.at[1, keep_part], (t, slab_of(-1))),
        ]
        for part, keep_part in (
            (slice(1, 1 + CHUNK // 2), slice(0, CHUNK // 2)),
            (slice(1 + CHUNK // 2, 1 + CHUNK), slice(CHUNK // 2, CHUNK)),
        )
    ]
    start_all(bulk[0])
    recv_all(to_slots)
    start_all(around)
    start_all(bulk[1])
    recv_all(around)

    nothing(1, 0)
    nothing(1, 7)
    win[:, 8:48, :] = means[0, 0]

    def corrected(phase, n, before):
        def extra(row, count):
            there = pl.ds(row - 8, 8, stride=count)
            return means[phase, n, :, there, :] - before[n, :, pl.ds(row, 8, stride=count), :]

        return extra

    def change(a, b):
        return lambda r: a[:, r : r + 8, :] - b[:, r : r + 8, :]

    for n in range(1, 7):
        coarse_step(-(-(44 - 4 * n) // 8), w_in, w_out, win, new.at[n], corrected(0, n, old), *scratch)
        keep(1, n, change(new.at[n], old.at[n]), 16)
    deliver_2 = out_copies(1, SLICES - 1, 16)
    start_all(deliver_2)
    keep_own(1, SLICES - 1)
    coarse_step(-(-(44 - 4 * 7) // 8), w_in, w_out, win, new.at[7], None, *scratch)

    for part in bulk:
        recv_all(part)
        sent_all(part)
    recv_all(deliver_2)

    @pl.when(t > 0)
    def _():
        coarse_in_chunks(got.at[1], coarse)

        def base(c, r):
            if r < 2:
                return edge[0, c, 8 * r : 8 * r + 8, :]
            if r >= 6:
                return edge[1, c, 8 * (r - 6) : 8 * (r - 6) + 8, :]
            return state[pl.ds(c.start + 1, 4), PAD + 8 * r : PAD + 8 * r + 8, :]

        spread_coarse(coarse, base, state)
        ghosts(state)
        fine_run(state, one, two, pcoef, qcoef, force)

    to_slots_2, around_2 = share_means(1, 0, (1, 7), (1, 3))
    load_own(state, lam)
    chunks_to_rows(lam, nat)
    recv_all(to_slots_2)
    start_all(around_2)
    recv_all(around_2)

    nothing(2, 0)
    nothing(2, 1)
    win[:, 8:48, :] = means[1, 1]
    for n in range(2, 8):
        coarse_step(
            -(-(40 - 4 * n) // 8), w_in, w_out, win, old.at[n], corrected(1, n, new) if n < 7 else None, *scratch
        )
        keep(2, n, change(old.at[n], new.at[n]), 8)
    deliver_3 = out_copies(2, 0, 8)
    start_all(deliver_3)
    keep_own(2, 0)
    recv_all(deliver_3)

    copies = jnp.where(
        lax.broadcasted_iota(jnp.int32, (LANES, 4 * LANES), 0)
        == lax.broadcasted_iota(jnp.int32, (LANES, 4 * LANES), 1) // 4, 1.0, 0.0,
    ).astype(F32)
    delta = jnp.concatenate([got[2, m // 2, m % 2, 0:8, :] for m in range(BLOCKS)], axis=0)
    packed[...] = jnp.dot(delta, copies, precision=HIGH, preferred_element_type=F32)
    for c in range(64):
        m, k = c // 4, c % 4
        v = packed[m * 8 : m * 8 + 8, k * LANES : (k + 1) * LANES]
        for q in range(4):
            at = pl.ds(c * PITCH + q, 8, stride=4)
            nat[at, :] = nat[at, :] + v
        out[:, c * LANES : (c + 1) * LANES] = nat[c * PITCH : c * PITCH + INNER, :]
    for group in (near, across, shared, deliver, to_slots, around, deliver_2, to_slots_2, around_2, deliver_3):
        sent_all(group)


def body(vorticity, stream, forcing, conv_in, conv_out):
    rows, cols = vorticity.shape
    whole = (CHUNK + 2, TALL, LANES)
    smem = pl.BlockSpec(memory_space=pltpu.SMEM)
    anywhere = pl.BlockSpec(memory_space=pl.ANY)
    window = (3, WINDOW, LANES)
    shapes = [
        (3, rows, cols), (64 * PITCH, LANES), (CHUNK * PITCH, LANES), (2,) + whole, whole, whole, whole, whole, whole,
        (4,) + whole, window, window, (SLICES,) + window, (SLICES,) + window,
        (9, 18, 8, LANES), (9, 18, 8, LANES), (3, 8, 3, 8, LANES), (8, 9, 8, LANES), (8, 9, 8, LANES),
        (3, BLOCKS + 2, 8, LANES), (2, SLICES, 3, 40, LANES), (3, SLICES, 2, 16, LANES), (3, SLICES, 2, 16, LANES),
        (2, CHUNK, HALO, LANES), (BLOCKS, 16, LANES), (8 * BLOCKS, 4 * LANES),
    ]
    out = pl.pallas_call(
        kernel,
        name="parareal",
        out_shape=jax.ShapeDtypeStruct((rows, cols), F32),
        in_specs=[smem, smem, anywhere, anywhere, anywhere],
        out_specs=pl.BlockSpec(memory_space=VMEM),
        scratch_shapes=[VMEM(s, F32) for s in shapes]
        + [pltpu.SemaphoreType.DMA((3,)), pltpu.SemaphoreType.DMA((SLOTS,)), pltpu.SemaphoreType.DMA((SLOTS,))],
        compiler_params=pltpu.CompilerParams(vmem_limit_bytes=62 * 2**20, collective_id=0, has_side_effects=True),
    )(conv_in, conv_out, vorticity, stream, forcing)
    return out[None]


def solution(mesh):
    placed = (P("space", None), P("space", None), P("space", None), P(), P())
    return jax.shard_map(
        body, mesh=mesh, in_specs=placed, out_specs=P("tm", "space", None), check_vma=False
    )
```

```python
import functools
import math

import jax
import jax.numpy as jnp
import numpy as np
from jax import lax
from jax.experimental import pallas as pl
from jax.experimental.pallas import tpu as pltpu
from jax.sharding import PartitionSpec as P

F32 = jnp.float32
VMEM = pltpu.VMEM
MESH = pl.DeviceIdType.MESH
HIGH = lax.Precision.HIGHEST

STEPS = 4
SLICES = 8
LANES = 128
CHUNK = 64
INNER = 32
HALO = 16
PAD = 8
TALL = INNER + 2 * HALO + 2 * PAD
OWN = PAD + HALO
PITCH = 33
BLOCKS = 16
REACH = 28
WINDOW = 2 * REACH


def fine_weights():
    shift = np.polynomial.Polynomial([-0.45, 0.2])
    of_w = sum(shift**j / math.factorial(j) for j in range(5))
    of_f = sum(shift**j / math.factorial(j + 1) for j in range(4))
    return [float(v) for v in of_w.coef], [float(v) for v in of_f.coef] + [0.0]


def lane_iota():
    return lax.broadcasted_iota(jnp.int32, (8, LANES), 1)


def lane_shifted(value, up):
    lane = lax.broadcasted_iota(jnp.int32, value.shape, 2)
    if up:
        rolled = pltpu.roll(value, LANES - 1, 2)
        return jnp.where(lane == LANES - 1, jnp.concatenate([rolled[1:], rolled[:1]], axis=0), rolled)
    rolled = pltpu.roll(value, 1, 2)
    return jnp.where(lane == 0, jnp.concatenate([rolled[-1:], rolled[:-1]], axis=0), rolled)


def lane_gather(value, index):
    return jnp.take_along_axis(value, index, axis=1)


def next_chunk():
    lane = lane_iota()
    return jnp.where(lane < 64, lane + 64, jnp.where(lane == 127, 0, lane - 63))


def previous_chunk():
    lane = lane_iota()
    return jnp.where(lane >= 64, lane - 64, jnp.where(lane == 0, 127, lane + 63))


def swap_tiles_and_lanes(tiles):
    lane = lane_iota()
    for bit in range(4):
        width = 4 << bit
        high = (lane // width) % 2 == 1
        out = list(tiles)
        for m in range(16):
            if not m >> bit & 1:
                a, b = tiles[m], tiles[m | 1 << bit]
                out[m] = jnp.where(high, pltpu.roll(b, width, 1), a)
                out[m | 1 << bit] = jnp.where(high, b, pltpu.roll(a, LANES - width, 1))
        tiles = out
    return tiles


def to_chunks(tiles):
    lane = lane_iota()
    index = ((lane % 4) * 2 + lane // 64) * 16 + (lane % 64) // 4
    return swap_tiles_and_lanes([lane_gather(t, index) for t in tiles])


def from_chunks(tiles):
    lane = lane_iota()
    block = lane // 16
    index = (block % 2) * 64 + (lane % 16) * 4 + block // 2
    return [lane_gather(t, index) for t in swap_tiles_and_lanes(tiles)]


def coarse_step(count, w_in, w_out, win, values, extra, taps, sums, parts):
    lanes = win.shape[0]
    off = REACH - 4 * count
    at = [pl.ds(off + q, 8, stride=count) for q in range(count)]

    def tiles(q):
        return slice(lanes * q, lanes * q + lanes)

    for q in range(count):
        x = win[:, at[q], :]
        for dx, v in enumerate((lane_shifted(x, False), x, lane_shifted(x, True))):
            for dy in range(3):
                place = q + 1 - dy
                if place < 0:
                    taps[dy * 3 + dx, tiles(count - 1)] = pltpu.roll(v, 7, 1)
                elif place >= count:
                    taps[dy * 3 + dx, tiles(0)] = pltpu.roll(v, 1, 1)
                else:
                    taps[dy * 3 + dx, tiles(place)] = v
    total = lanes * count
    group = GROUP

    def few(i, _):
        some = pl.ds(jnp.minimum(i * group, total - group), group)
        x = taps[:, some]
        acc = None
        for h in range(8):
            hidden = jnp.tanh(jnp.sum(w_in[h][:, None] * x, axis=0))
            term = w_out[h][:, None] * hidden[None]
            acc = term if acc is None else acc + term
        sums[:, some] = acc
        return 0

    lax.fori_loop(0, -(-total // group), few, 0)
    for q in range(count):
        for dy in range(3):
            low = lane_shifted(sums[dy * 3, tiles(q)], False)
            high = lane_shifted(sums[dy * 3 + 2, tiles(q)], True)
            v = low + high + sums[dy * 3 + 1, tiles(q)]
            parts[dy, q + 1] = v
            if q == 0 and dy == 2:
                parts[dy, count + 1] = pltpu.roll(v, 7, 1)
            if q == count - 1 and dy == 0:
                parts[dy, 0] = pltpu.roll(v, 1, 1)
    for q in range(count):
        g = win[:, at[q], :] + (parts[0, q] + parts[1, q + 1] + parts[2, q + 2])
        values[:, at[q], :] = g
        if extra is not None:
            win[:, at[q], :] = g + extra(off + q, count)


def own_columns(value):
    rolled = pltpu.roll(value, 64, 2)
    lane = lax.broadcasted_iota(jnp.int32, (2, 8, LANES), 2)
    return jnp.where(lane < 64, rolled[:2], rolled[1:])


def fine_stage(src, dst, base, pcoef, qcoef, force, off, count, scale, of_base):
    at = [pl.ds(off + q, 8, stride=count) for q in range(-1, count + 1)]

    def block(first, size):
        centre = pl.ds(first, size)
        wide = [src[pl.ds(first - 1, size + 2), a, :] for a in at[1:-1]]
        column = [src[centre, at[0], :]] + [x[1:-1] for x in wide] + [src[centre, at[-1], :]]
        results = []
        for q in range(count):
            slot = (centre, at[q + 1], slice(None))
            left, right = wide[q][:-2], wide[q][2:]
            above, below = column[q + 2], column[q]
            t = pcoef[slot] * (right - left) + qcoef[slot] * (above - below) + (left + below)
            if scale != 1.0:
                t = scale * t
            here = column[q + 1] if src is base else base[slot]
            t = t + (of_base * here + force[slot])
            dst[slot] = t
            results.append(t)
        return results

    last = block(CHUNK - 1, 2)
    first = block(1, 2)
    ahead, back = next_chunk(), previous_chunk()
    for q in range(count):
        dst[0, at[q + 1], :] = lane_gather(last[q][1], back)
        dst[CHUNK + 1, at[q + 1], :] = lane_gather(first[q][0], ahead)
    group = 6 if count > 6 else 10

    def body(g, _):
        block(3 + g * group, group)
        return 0

    lax.fori_loop(0, (CHUNK - 4) // group, body, 0)


def fine_run(state, one, two, pcoef, qcoef, force):
    of_w, _ = fine_weights()
    for step in range(STEPS):
        count = 9 if step == 0 else 8 - step
        off = 4 if step == 0 else PAD + 4 * step
        shared = (state, pcoef, qcoef)
        fine_stage(state, one, *shared, force.at[3], off, count, 1.0, of_w[3] / of_w[4])
        fine_stage(one, two, *shared, force.at[2], off, count, 1.0, of_w[2] / of_w[4])
        fine_stage(two, one, *shared, force.at[1], off, count, 1.0, of_w[1] / of_w[4])
        fine_stage(one, state, *shared, force.at[0], off, count, of_w[4], of_w[0])


def ghosts(ref):
    ahead, back = next_chunk(), previous_chunk()
    for r in range(PAD, TALL - PAD, 8):
        ref[0, r : r + 8, :] = lane_gather(ref[CHUNK, r : r + 8, :], back)
        ref[CHUNK + 1, r : r + 8, :] = lane_gather(ref[1, r : r + 8, :], ahead)


def coefficients(stream, forcing, pcoef, qcoef, force):
    of_w, of_f = fine_weights()
    ghosts(stream)
    count = 9
    at = [pl.ds(4 + q, 8, stride=count) for q in range(-1, count + 1)]

    group = 4

    def body(g, _):
        first = 1 + g * group
        c = pl.ds(first, group)
        wide = [stream[pl.ds(first - 1, group + 2), a, :] for a in at[1:-1]]
        x = [stream[c, at[0], :]] + [v[1:-1] for v in wide] + [stream[c, at[-1], :]]
        for q in range(count):
            a = at[q + 1]
            pcoef[c, a, :] = 0.5 - 1.25 * (x[q + 2] - x[q])
            qcoef[c, a, :] = 0.5 + 1.25 * (wide[q][2:] - wide[q][:-2])
            f = forcing[c, a, :]
            force[0, c, a, :] = of_f[0] * f
            for k in range(1, 4):
                force[k, c, a, :] = (of_f[k] / of_w[4]) * f
        return 0

    lax.fori_loop(0, CHUNK // group, body, 0)


def natural_to_rows(source, nat):
    for c in range(64):
        nat[c * PITCH : c * PITCH + INNER, :] = source[:, c * LANES : (c + 1) * LANES]


def rows_to_chunks(nat, lam):
    low = lax.broadcasted_iota(jnp.int32, (64, LANES), 1) < 64
    for i in range(INNER // 2):
        j = i + INNER // 2
        at_i, at_j = pl.ds(i, 64, stride=PITCH), pl.ds(j, 64, stride=PITCH)
        flipped = jnp.concatenate([nat[at_i, :], nat[at_j, :]], axis=0).T
        top, bottom = flipped[:64], flipped[64:]
        lam[at_i, :] = jnp.where(low, top, pltpu.roll(bottom, 64, 1))
        lam[at_j, :] = jnp.where(low, pltpu.roll(top, 64, 1), bottom)


def chunks_to_rows(lam, nat):
    low = lax.broadcasted_iota(jnp.int32, (64, LANES), 1) < 64
    for i in range(INNER // 2):
        j = i + INNER // 2
        at_i, at_j = pl.ds(i, 64, stride=PITCH), pl.ds(j, 64, stride=PITCH)
        x, y = lam[at_i, :], lam[at_j, :]
        top = jnp.where(low, x, pltpu.roll(y, 64, 1))
        bottom = jnp.where(low, pltpu.roll(x, 64, 1), y)
        flipped = jnp.concatenate([top, bottom], axis=0).T
        nat[at_i, :] = flipped[:64]
        nat[at_j, :] = flipped[64:]


def store_own(lam, ref):
    for c in range(CHUNK):
        ref[1 + c, OWN : OWN + INNER, :] = lam[c * PITCH : c * PITCH + INNER, :]


def load_own(ref, lam):
    for c in range(CHUNK):
        lam[c * PITCH : c * PITCH + INNER, :] = ref[1 + c, OWN : OWN + INNER, :]


def spaced_tiles(tiles, rolled):
    lane = lane_iota()
    turned = [pltpu.roll(t, 64, 1) for t in tiles]
    for k in range(BLOCKS):
        v = jnp.where(lane < 64, turned[k - 1], turned[k])
        rolled[k] = v
        if k < 2:
            rolled[BLOCKS + k] = v


def block_means(state):
    tiles = []
    for m in range(BLOCKS):
        four = [state[1 + 4 * m : 5 + 4 * m, pl.ds(OWN + q, 8, stride=4), :] for q in range(4)]
        tiles.append(0.0625 * jnp.sum((four[0] + four[1]) + (four[2] + four[3]), axis=0))
    return from_chunks(tiles)


def coarse_in_chunks(pieces, coarse):
    for half in range(2):
        at = pl.ds(half, 8, stride=2)
        tiles = to_chunks([pieces[m // 2, m % 2, at, :] for m in range(BLOCKS)])
        for m in range(BLOCKS):
            coarse[m, at, :] = tiles[m]


def spread_coarse(coarse, base, state):
    upper = lax.broadcasted_iota(jnp.int32, (8, LANES), 0) < 4

    def body(m, _):
        c = pl.ds(4 * m, 4)
        for r in range(8):
            v = jnp.where(upper, coarse[m, 2 * r : 2 * r + 1, :], coarse[m, 2 * r + 1 : 2 * r + 2, :])[None]
            old = base(c, r)
            v = jnp.broadcast_to(v, (4, 8, LANES)) if old is None else old + v
            state[pl.ds(4 * m + 1, 4), PAD + 8 * r : PAD + 8 * r + 8, :] = v
        return 0

    lax.fori_loop(0, BLOCKS, body, 0)


GROUP = 2


def kernel(
    conv_in, conv_out, vort_hbm, stream_hbm, force_hbm, out, delta_out,
    inputs, nat, lam, fields, state, one, two, pcoef, qcoef, force,
    start, win, old, new, taps, sums, parts, w_in, w_out,
    rolled, means, sent, got, edge, coarse, packed,
    in_sem, send_sem, recv_sem,
):
    t, z = lax.axis_index("tm"), lax.axis_index("space")
    slabs = lax.axis_size("space")
    parity = lax.rem(t, 2)
    used = [0]

    def slot_of(k):
        return lax.rem(t + k, SLICES)

    def slab_of(d):
        return lax.rem(z + d + slabs, slabs)

    def reserve(count):
        used[0] += count
        return used[0] - count

    def remote(src, dst, to, send=None, recv=None):
        if send is None:
            send = recv = reserve(1)
        return pltpu.make_async_remote_copy(
            src_ref=src, dst_ref=dst, send_sem=send_sem.at[send], recv_sem=recv_sem.at[recv],
            device_id=to, device_id_type=MESH,
        )

    def start_all(copies):
        for c in copies:
            c.start()

    def recv_all(copies):
        for c in copies:
            c.wait_recv()

    def sent_all(copies):
        for c in copies:
            c.wait_send()

    loads = [
        pltpu.make_async_copy(ref, inputs.at[i], in_sem.at[i])
        for i, ref in enumerate((vort_hbm, stream_hbm, force_hbm))
    ]
    start_all(loads)
    barrier = pltpu.get_barrier_semaphore()
    peers = [(slot_of(k), z) for k in range(1, SLICES)] + [(t, slab_of(d)) for d in (-3, -2, -1, 1, 2, 3)]
    for p in peers:
        pl.semaphore_signal(barrier, inc=1, device_id=p, device_id_type=MESH)
    for h in range(8):
        v_in, v_out = conv_in[h], 0.5 * conv_out[h]
        for k in range(9):
            one_value = (slice(k // 3, k // 3 + 1), slice(k % 3, k % 3 + 1))
            w_in[h, k] = jnp.broadcast_to(v_in[one_value], (8, LANES))
            w_out[h, k] = jnp.broadcast_to(v_out[one_value], (8, LANES))

    loads[0].wait()
    natural_to_rows(inputs.at[0], nat)
    for c in range(64):
        four = [nat[pl.ds(c * PITCH + q, 8, stride=4), :] for q in range(4)]
        m, k = c // 4, c % 4
        packed[m * 8 : m * 8 + 8, k * LANES : (k + 1) * LANES] = (four[0] + four[1]) + (four[2] + four[3])
    averages = jnp.where(
        lax.broadcasted_iota(jnp.int32, (4 * LANES, LANES), 0) // 4
        == lax.broadcasted_iota(jnp.int32, (4 * LANES, LANES), 1), 0.0625, 0.0,
    ).astype(F32)
    first = jnp.dot(packed[...], averages, precision=HIGH, preferred_element_type=F32)
    spaced_tiles([first[m * 8 : m * 8 + 8] for m in range(BLOCKS)], rolled.at[0])
    mine = pl.ds(2 * t, 3)
    pl.semaphore_wait(barrier, len(peers))
    near = [
        remote(rolled.at[0, mine], start.at[:, REACH - 4 - 8 * d : REACH + 4 - 8 * d, :], (t, slab_of(d)))
        for d in (-1, 1, -2, 2, -3, 3)
    ]
    start_all(near)
    start[:, REACH - 4 : REACH + 4, :] = rolled[0, mine]

    @pl.when(t == 1)
    def _():
        rows_to_chunks(nat, lam)
        store_own(lam, state)

    inside = slice(1, CHUNK + 1)
    halves = [slice(1, 1 + CHUNK // 2), slice(1 + CHUNK // 2, 1 + CHUNK)]
    low, high = slice(OWN - HALO, OWN), slice(OWN + INNER, OWN + INNER + HALO)
    first_rows, last_rows = slice(OWN, OWN + HALO), slice(OWN + INNER - HALO, OWN + INNER)
    sibling = (t + 1 - 2 * parity, z)
    across, shared = [], []
    for part in halves:
        across.append(
            [
                remote(fields.at[parity, part, last_rows], fields.at[parity, part, low], (t, slab_of(1))),
                remote(fields.at[parity, part, first_rows], fields.at[parity, part, high], (t, slab_of(-1))),
            ]
        )
        shared.append(
            [remote(fields.at[parity, part, rows], fields.at[parity, part, rows], sibling) for rows in (low, high)]
        )
    early = [
        remote(state.at[inside, last_rows], state.at[inside, low], (t, slab_of(1))),
        remote(state.at[inside, first_rows], state.at[inside, high], (t, slab_of(-1))),
    ]
    loads[1].wait()
    loads[2].wait()
    for turn in range(2):
        which = parity if turn == 0 else 1 - parity
        natural_to_rows(inputs.at[1 + which], nat)
        rows_to_chunks(nat, lam)
        store_own(lam, fields.at[which])
        if turn == 0:
            start_all(across[0])
            start_all(across[1])

    @pl.when(t == 1)
    def _():
        start_all(early)

    recv_all(near)
    win[...] = start[...]
    scratch = (taps, sums, parts)

    def rows_of(ref):
        return lambda r: ref[:, r : r + 8, :]

    def change(a, b):
        return lambda r: a[:, r : r + 8, :] - b[:, r : r + 8, :]

    def deliverer(phase, rows):
        send, recv = reserve(SLICES), reserve(SLICES)
        here = slice(0, rows)

        def copy(n, to, source):
            return remote(
                sent.at[phase, n, :, here], got.at[phase, source, :, here], (to, z), send + n, recv + source
            )

        def put(n, to, read):
            for r in range(0, rows, 8):
                sent[phase, n, :, r : r + 8, :] = own_columns(read(REACH - rows // 2 + r))

            @pl.when(t != to)
            def _():
                copy(n, to, t).start()

            @pl.when(t == to)
            def _():
                got[phase, t, :, here, :] = sent[phase, n, :, here, :]

        def take():
            @pl.when(t > 1)
            def _():
                for k in range(1, SLICES):
                    copy(2, 2, slot_of(k)).wait_recv()

        def done(pairs):
            for n, to in pairs:
                @pl.when(t != to)
                def _():
                    copy(n, to, t).wait_send()

        return put, take, done

    plain = lambda row, count: 0.0
    put_0, take_0, done_0 = deliverer(0, 16)
    for n in range(8):
        coarse_step(-(-(44 - 4 * n) // 8), w_in, w_out, win, old.at[n], plain if n < 7 else None, *scratch)
        if n < 6:
            put_0(n + 1, n + 2, rows_of(win))

    for part in range(2):
        recv_all(across[part])
        start_all(shared[part])
    for part in range(2):
        recv_all(shared[part])
    coefficients(fields.at[0], fields.at[1], pcoef, qcoef, force)
    take_0()

    @pl.when(t == 1)
    def _():
        recv_all(early)
        sent_all(early)

    @pl.when(t > 1)
    def _():
        coarse_in_chunks(got.at[0], coarse)
        spread_coarse(coarse, lambda c, r: None, state)

    @pl.when(t > 0)
    def _():
        ghosts(state)
        fine_run(state, one, two, pcoef, qcoef, force)

    def sharer(phase, shift, wanted, wanted_two):
        place = lax.rem(t + shift, SLICES)
        middle = slice(16, 24)
        send, recv, around = reserve(SLICES), reserve(SLICES), reserve(4 * SLICES)

        def copy(k, slot):
            return remote(
                rolled.at[phase + 1, pl.ds(2 * slot_of(k), 3)], means.at[phase, slot, :, middle],
                (slot_of(k), z), send + k, recv + slot,
            )

        def spread(n):
            return [
                remote(
                    means.at[phase, n, :, middle], means.at[phase, n, :, 16 - 8 * d : 24 - 8 * d],
                    (t, slab_of(d)), around + 4 * n + j, around + 4 * n + j,
                )
                for j, d in enumerate((-1, 1, -2, 2))
                if abs(d) == 1 or n in wanted_two
            ]

        has_slice = functools.reduce(jnp.logical_or, [place == n for n in wanted])

        def go():
            @pl.when(has_slice)
            def _():
                spaced_tiles(block_means(state), rolled.at[phase + 1])
                for k in range(1, SLICES):
                    copy(k, place).start()
                means[phase, place, :, middle, :] = rolled[phase + 1, pl.ds(2 * t, 3)]

        def pass_on():
            for n in wanted:
                @pl.when(place != n)
                def _():
                    copy(1, n).wait_recv()

                start_all(spread(n))

        def take(n):
            recv_all(spread(n))

        def done():
            @pl.when(has_slice)
            def _():
                for k in range(1, SLICES):
                    copy(k, place).wait_send()

            for n in wanted:
                sent_all(spread(n))

        return go, pass_on, take, done

    go_1, pass_1, arrived_1, shared_1 = sharer(0, SLICES - 1, range(0, 7), range(0, 4))
    go_1()
    copy_f = remote(state.at[inside, slice(OWN, OWN + INNER)], one.at[inside, slice(OWN, OWN + INNER)], (0, z))

    @pl.when(t == 1)
    def _():
        copy_f.start()

    pass_1()
    bulk = [
        remote(state.at[inside, last_rows], edge.at[0], (t, slab_of(1))),
        remote(state.at[inside, first_rows], edge.at[1], (t, slab_of(-1))),
    ]

    @pl.when(t > 0)
    def _():
        start_all(bulk)

    def corrected(phase, n, before):
        def extra(row, count):
            there = pl.ds(row - 8, 8, stride=count)
            return means[phase, n, :, there, :] - before[n, :, pl.ds(row, 8, stride=count), :]

        return extra

    put_1, take_1, done_1 = deliverer(1, 16)
    arrived_1(0)
    win[:, 8:48, :] = means[0, 0]
    for n in range(1, 8):
        if n < 7:
            arrived_1(n)
        coarse_step(
            -(-(44 - 4 * n) // 8), w_in, w_out, win, new.at[n], corrected(0, n, old) if n < 7 else None, *scratch
        )
        if n < 7:
            put_1(n, n + 1, change(new.at[n], old.at[n]))

    take_1()

    @pl.when(t == 1)
    def _():
        copy_f.wait_send()
        got[1] = jnp.zeros(got.shape[1:], F32)

    @pl.when(t > 0)
    def _():
        recv_all(bulk)
        sent_all(bulk)
        coarse_in_chunks(got.at[1], coarse)

        def base(c, r):
            if r < 2:
                return edge[0, c, 8 * r : 8 * r + 8, :]
            if r >= 6:
                return edge[1, c, 8 * (r - 6) : 8 * (r - 6) + 8, :]
            return state[pl.ds(c.start + 1, 4), PAD + 8 * r : PAD + 8 * r + 8, :]

        spread_coarse(coarse, base, state)
        ghosts(state)
        fine_run(state, one, two, pcoef, qcoef, force)

    go_2, pass_2, arrived_2, shared_2 = sharer(1, 0, range(1, 7), range(1, 3))
    go_2()
    pass_2()

    @pl.when(t == 0)
    def _():
        copy_f.wait_recv()
        load_own(one, lam)

    @pl.when(t > 0)
    def _():
        load_own(state, lam)

    put_2, take_2, done_2 = deliverer(2, 8)
    arrived_2(1)
    win[:, 8:48, :] = means[1, 1]
    for n in range(2, 8):
        if n < 7:
            arrived_2(n)
        coarse_step(
            -(-(40 - 4 * n) // 8), w_in, w_out, win, old.at[n], corrected(1, n, new) if n < 7 else None, *scratch
        )
        put_2(n, n, change(old.at[n], new.at[n]))

    chunks_to_rows(lam, nat)
    for c in range(64):
        out[:, c * LANES : (c + 1) * LANES] = nat[c * PITCH : c * PITCH + INNER, :]

    @pl.when(t <= 1)
    def _():
        got[2] = jnp.zeros(got.shape[1:], F32)

    sent_all(near)
    for part in range(2):
        sent_all(across[part])
        sent_all(shared[part])
    done_0([(n, n + 1) for n in range(1, 7)])
    done_1([(n, n + 1) for n in range(1, 7)])
    done_2([(n, n) for n in range(2, 8)])
    shared_1()
    shared_2()
    take_2()
    for m in range(BLOCKS):
        delta_out[m * 8 : m * 8 + 8, :] = got[2, m // 2, m % 2, 0:8, :]


def finish_kernel(fine, delta, out):
    copies = jnp.where(
        lax.broadcasted_iota(jnp.int32, (LANES, 4 * LANES), 0)
        == lax.broadcasted_iota(jnp.int32, (LANES, 4 * LANES), 1) // 4, 1.0, 0.0,
    ).astype(F32)
    wide = jnp.dot(delta[...], copies, precision=HIGH, preferred_element_type=F32)
    upper = lax.broadcasted_iota(jnp.int32, (8, 4 * LANES), 0) < 4
    for m in range(delta.shape[0] // 8):
        cols = slice(m * 4 * LANES, (m + 1) * 4 * LANES)
        for a in range(INNER // 8):
            r = m * 8 + 2 * a
            v = jnp.where(upper, wide[r : r + 1], wide[r + 1 : r + 2])
            out[0, a * 8 : a * 8 + 8, cols] = fine[a * 8 : a * 8 + 8, cols] + v


def body(vorticity, stream, forcing, conv_in, conv_out):
    rows, cols = vorticity.shape
    whole = (CHUNK + 2, TALL, LANES)
    vmem = pl.BlockSpec(memory_space=VMEM)
    anywhere = pl.BlockSpec(memory_space=pl.ANY)
    window = (3, WINDOW, LANES)
    shapes = [
        (3, rows, cols), (64 * PITCH, LANES), (CHUNK * PITCH, LANES), (2,) + whole, whole, whole, whole, whole, whole,
        (4,) + whole, window, window, (SLICES,) + window, (SLICES,) + window,
        (9, 18, 8, LANES), (9, 18, 8, LANES), (3, 8, 3, 8, LANES), (8, 9, 8, LANES), (8, 9, 8, LANES),
        (3, BLOCKS + 2, 8, LANES), (2, SLICES, 3, 40, LANES), (3, SLICES, 2, 16, LANES), (3, SLICES, 2, 16, LANES),
        (2, CHUNK, HALO, LANES), (BLOCKS, 16, LANES), (8 * BLOCKS, 4 * LANES),
    ]
    slots = 176
    fine, delta = pl.pallas_call(
        kernel,
        name="parareal",
        out_shape=(jax.ShapeDtypeStruct((rows, cols), F32), jax.ShapeDtypeStruct((8 * BLOCKS, LANES), F32)),
        in_specs=[vmem, vmem, anywhere, anywhere, anywhere],
        out_specs=(vmem, vmem),
        scratch_shapes=[VMEM(s, F32) for s in shapes]
        + [pltpu.SemaphoreType.DMA((3,)), pltpu.SemaphoreType.DMA((slots,)), pltpu.SemaphoreType.DMA((slots,))],
        compiler_params=pltpu.CompilerParams(vmem_limit_bytes=62 * 2**20, collective_id=0, has_side_effects=True),
    )(conv_in, conv_out, vorticity, stream, forcing)
    grid = 4
    return pl.pallas_call(
        finish_kernel,
        name="finish",
        grid=(grid,),
        out_shape=jax.ShapeDtypeStruct((1, rows, cols), F32),
        in_specs=[
            pl.BlockSpec((rows, cols // grid), lambda i: (0, i)),
            pl.BlockSpec((8 * BLOCKS // grid, LANES), lambda i: (i, 0)),
        ],
        out_specs=pl.BlockSpec((1, rows, cols // grid), lambda i: (0, 0, i)),
    )(fine, delta)


def solution(mesh):
    placed = (P("space", None), P("space", None), P("space", None), P(), P())
    return jax.shard_map(
        body, mesh=mesh, in_specs=placed, out_specs=P("tm", "space", None), check_vma=False
    )
```

```python
import functools
import math

import jax
import jax.numpy as jnp
import numpy as np
from jax import lax
from jax.experimental import pallas as pl
from jax.experimental.pallas import tpu as pltpu
from jax.sharding import PartitionSpec as P

F32 = jnp.float32
VMEM = pltpu.VMEM
MESH = pl.DeviceIdType.MESH
HIGH = lax.Precision.HIGHEST

STEPS = 4
SLICES = 8
LANES = 128
CHUNK = 64
INNER = 32
HALO = 16
PAD = 8
TALL = INNER + 2 * HALO + 2 * PAD
OWN = PAD + HALO
PITCH = 33
BLOCKS = 16
REACH = 28
WINDOW = 2 * REACH


def fine_weights():
    shift = np.polynomial.Polynomial([-0.45, 0.2])
    of_w = sum(shift**j / math.factorial(j) for j in range(5))
    of_f = sum(shift**j / math.factorial(j + 1) for j in range(4))
    return [float(v) for v in of_w.coef], [float(v) for v in of_f.coef] + [0.0]


def lane_iota():
    return lax.broadcasted_iota(jnp.int32, (8, LANES), 1)


def lane_shifted(value, up):
    lane = lax.broadcasted_iota(jnp.int32, value.shape, 2)
    if up:
        rolled = pltpu.roll(value, LANES - 1, 2)
        return jnp.where(lane == LANES - 1, jnp.concatenate([rolled[1:], rolled[:1]], axis=0), rolled)
    rolled = pltpu.roll(value, 1, 2)
    return jnp.where(lane == 0, jnp.concatenate([rolled[-1:], rolled[:-1]], axis=0), rolled)


def lane_gather(value, index):
    return jnp.take_along_axis(value, index, axis=1)


def next_chunk():
    lane = lane_iota()
    return jnp.where(lane < 64, lane + 64, jnp.where(lane == 127, 0, lane - 63))


def previous_chunk():
    lane = lane_iota()
    return jnp.where(lane >= 64, lane - 64, jnp.where(lane == 0, 127, lane + 63))


def swap_tiles_and_lanes(tiles):
    lane = lane_iota()
    for bit in range(4):
        width = 4 << bit
        high = (lane // width) % 2 == 1
        out = list(tiles)
        for m in range(16):
            if not m >> bit & 1:
                a, b = tiles[m], tiles[m | 1 << bit]
                out[m] = jnp.where(high, pltpu.roll(b, width, 1), a)
                out[m | 1 << bit] = jnp.where(high, b, pltpu.roll(a, LANES - width, 1))
        tiles = out
    return tiles


def to_chunks(tiles):
    lane = lane_iota()
    index = ((lane % 4) * 2 + lane // 64) * 16 + (lane % 64) // 4
    return swap_tiles_and_lanes([lane_gather(t, index) for t in tiles])


def from_chunks(tiles):
    lane = lane_iota()
    block = lane // 16
    index = (block % 2) * 64 + (lane % 16) * 4 + block // 2
    return [lane_gather(t, index) for t in swap_tiles_and_lanes(tiles)]


def coarse_step(count, w_in, w_out, win, values, extra, taps, sums, parts):
    lanes = win.shape[0]
    off = REACH - 4 * count
    at = [pl.ds(off + q, 8, stride=count) for q in range(count)]

    def tiles(q):
        return slice(lanes * q, lanes * q + lanes)

    for q in range(count):
        x = win[:, at[q], :]
        for dx, v in enumerate((lane_shifted(x, False), x, lane_shifted(x, True))):
            for dy in range(3):
                place = q + 1 - dy
                if place < 0:
                    taps[dy * 3 + dx, tiles(count - 1)] = pltpu.roll(v, 7, 1)
                elif place >= count:
                    taps[dy * 3 + dx, tiles(0)] = pltpu.roll(v, 1, 1)
                else:
                    taps[dy * 3 + dx, tiles(place)] = v
    total = lanes * count
    group = GROUP

    def few(i, _):
        some = pl.ds(jnp.minimum(i * group, total - group), group)
        x = taps[:, some]
        acc = None
        for h in range(8):
            hidden = jnp.tanh(jnp.sum(w_in[h][:, None] * x, axis=0))
            term = w_out[h][:, None] * hidden[None]
            acc = term if acc is None else acc + term
        sums[:, some] = acc
        return 0

    lax.fori_loop(0, -(-total // group), few, 0)
    for q in range(count):
        for dy in range(3):
            low = lane_shifted(sums[dy * 3, tiles(q)], False)
            high = lane_shifted(sums[dy * 3 + 2, tiles(q)], True)
            v = low + high + sums[dy * 3 + 1, tiles(q)]
            parts[dy, q + 1] = v
            if q == 0 and dy == 2:
                parts[dy, count + 1] = pltpu.roll(v, 7, 1)
            if q == count - 1 and dy == 0:
                parts[dy, 0] = pltpu.roll(v, 1, 1)
    for q in range(count):
        g = win[:, at[q], :] + (parts[0, q] + parts[1, q + 1] + parts[2, q + 2])
        values[:, at[q], :] = g
        if extra is not None:
            win[:, at[q], :] = g + extra(off + q, count)


def own_columns(value):
    rolled = pltpu.roll(value, 64, 2)
    lane = lax.broadcasted_iota(jnp.int32, (2, 8, LANES), 2)
    return jnp.where(lane < 64, rolled[:2], rolled[1:])


def fine_stage(src, dst, base, pcoef, qcoef, force, off, count, scale, of_base):
    at = [pl.ds(off + q, 8, stride=count) for q in range(-1, count + 1)]

    def block(first, size):
        centre = pl.ds(first, size)
        wide = [src[pl.ds(first - 1, size + 2), a, :] for a in at[1:-1]]
        column = [src[centre, at[0], :]] + [x[1:-1] for x in wide] + [src[centre, at[-1], :]]
        results = []
        for q in range(count):
            slot = (centre, at[q + 1], slice(None))
            left, right = wide[q][:-2], wide[q][2:]
            above, below = column[q + 2], column[q]
            t = pcoef[slot] * (right - left) + qcoef[slot] * (above - below) + (left + below)
            if scale != 1.0:
                t = scale * t
            here = column[q + 1] if src is base else base[slot]
            t = t + (of_base * here + force[slot])
            dst[slot] = t
            results.append(t)
        return results

    last = block(CHUNK - 1, 2)
    first = block(1, 2)
    ahead, back = next_chunk(), previous_chunk()
    for q in range(count):
        dst[0, at[q + 1], :] = lane_gather(last[q][1], back)
        dst[CHUNK + 1, at[q + 1], :] = lane_gather(first[q][0], ahead)
    group = 6 if count > 6 else 10

    def body(g, _):
        block(3 + g * group, group)
        return 0

    lax.fori_loop(0, (CHUNK - 4) // group, body, 0)


def fine_run(state, one, two, pcoef, qcoef, force):
    of_w, _ = fine_weights()
    for step in range(STEPS):
        count = 9 if step == 0 else 8 - step
        off = 4 if step == 0 else PAD + 4 * step
        shared = (state, pcoef, qcoef)
        fine_stage(state, one, *shared, force.at[3], off, count, 1.0, of_w[3] / of_w[4])
        fine_stage(one, two, *shared, force.at[2], off, count, 1.0, of_w[2] / of_w[4])
        fine_stage(two, one, *shared, force.at[1], off, count, 1.0, of_w[1] / of_w[4])
        fine_stage(one, state, *shared, force.at[0], off, count, of_w[4], of_w[0])


def ghosts(ref):
    ahead, back = next_chunk(), previous_chunk()
    for r in range(PAD, TALL - PAD, 8):
        ref[0, r : r + 8, :] = lane_gather(ref[CHUNK, r : r + 8, :], back)
        ref[CHUNK + 1, r : r + 8, :] = lane_gather(ref[1, r : r + 8, :], ahead)


def coefficients(stream, forcing, pcoef, qcoef, force):
    of_w, of_f = fine_weights()
    ghosts(stream)
    count = 9
    at = [pl.ds(4 + q, 8, stride=count) for q in range(-1, count + 1)]

    group = 4

    def body(g, _):
        first = 1 + g * group
        c = pl.ds(first, group)
        wide = [stream[pl.ds(first - 1, group + 2), a, :] for a in at[1:-1]]
        x = [stream[c, at[0], :]] + [v[1:-1] for v in wide] + [stream[c, at[-1], :]]
        for q in range(count):
            a = at[q + 1]
            pcoef[c, a, :] = 0.5 - 1.25 * (x[q + 2] - x[q])
            qcoef[c, a, :] = 0.5 + 1.25 * (wide[q][2:] - wide[q][:-2])
            f = forcing[c, a, :]
            force[0, c, a, :] = of_f[0] * f
            for k in range(1, 4):
                force[k, c, a, :] = (of_f[k] / of_w[4]) * f
        return 0

    lax.fori_loop(0, CHUNK // group, body, 0)


def natural_to_rows(source, nat):
    for c in range(64):
        nat[c * PITCH : c * PITCH + INNER, :] = source[:, c * LANES : (c + 1) * LANES]


def rows_to_chunks(nat, lam):
    low = lax.broadcasted_iota(jnp.int32, (64, LANES), 1) < 64
    for i in range(INNER // 2):
        j = i + INNER // 2
        at_i, at_j = pl.ds(i, 64, stride=PITCH), pl.ds(j, 64, stride=PITCH)
        flipped = jnp.concatenate([nat[at_i, :], nat[at_j, :]], axis=0).T
        top, bottom = flipped[:64], flipped[64:]
        lam[at_i, :] = jnp.where(low, top, pltpu.roll(bottom, 64, 1))
        lam[at_j, :] = jnp.where(low, pltpu.roll(top, 64, 1), bottom)


def chunks_to_rows(lam, nat):
    low = lax.broadcasted_iota(jnp.int32, (64, LANES), 1) < 64
    for i in range(INNER // 2):
        j = i + INNER // 2
        at_i, at_j = pl.ds(i, 64, stride=PITCH), pl.ds(j, 64, stride=PITCH)
        x, y = lam[at_i, :], lam[at_j, :]
        top = jnp.where(low, x, pltpu.roll(y, 64, 1))
        bottom = jnp.where(low, pltpu.roll(x, 64, 1), y)
        flipped = jnp.concatenate([top, bottom], axis=0).T
        nat[at_i, :] = flipped[:64]
        nat[at_j, :] = flipped[64:]


def store_own(lam, ref):
    for c in range(CHUNK):
        ref[1 + c, OWN : OWN + INNER, :] = lam[c * PITCH : c * PITCH + INNER, :]


def load_own(ref, lam):
    for c in range(CHUNK):
        lam[c * PITCH : c * PITCH + INNER, :] = ref[1 + c, OWN : OWN + INNER, :]


def spaced_tiles(tiles, rolled):
    lane = lane_iota()
    turned = [pltpu.roll(t, 64, 1) for t in tiles]
    for k in range(BLOCKS):
        v = jnp.where(lane < 64, turned[k - 1], turned[k])
        rolled[k] = v
        if k < 2:
            rolled[BLOCKS + k] = v


def block_means(state):
    tiles = []
    for m in range(BLOCKS):
        four = [state[1 + 4 * m : 5 + 4 * m, pl.ds(OWN + q, 8, stride=4), :] for q in range(4)]
        tiles.append(0.0625 * jnp.sum((four[0] + four[1]) + (four[2] + four[3]), axis=0))
    return from_chunks(tiles)


def coarse_in_chunks(pieces, coarse):
    for half in range(2):
        at = pl.ds(half, 8, stride=2)
        tiles = to_chunks([pieces[m // 2, m % 2, at, :] for m in range(BLOCKS)])
        for m in range(BLOCKS):
            coarse[m, at, :] = tiles[m]


def spread_coarse(coarse, base, state):
    upper = lax.broadcasted_iota(jnp.int32, (8, LANES), 0) < 4

    def body(m, _):
        c = pl.ds(4 * m, 4)
        for r in range(8):
            v = jnp.where(upper, coarse[m, 2 * r : 2 * r + 1, :], coarse[m, 2 * r + 1 : 2 * r + 2, :])[None]
            old = base(c, r)
            v = jnp.broadcast_to(v, (4, 8, LANES)) if old is None else old + v
            state[pl.ds(4 * m + 1, 4), PAD + 8 * r : PAD + 8 * r + 8, :] = v
        return 0

    lax.fori_loop(0, BLOCKS, body, 0)


GROUP = 2
MIDWAY = 3
AHEAD = 24


def kernel(
    conv_in, conv_out, vort_hbm, stream_hbm, force_hbm, out, delta_out,
    inputs, nat, lam, fields, state, one, two, pcoef, qcoef, force,
    start, win, old, new, taps, sums, parts, w_in, w_out,
    rolled, means, sent, got, edge, coarse, packed,
    in_sem, send_sem, recv_sem,
):
    t, z = lax.axis_index("tm"), lax.axis_index("space")
    slabs = lax.axis_size("space")
    parity = lax.rem(t, 2)
    used = [0]

    def slot_of(k):
        return lax.rem(t + k, SLICES)

    def slab_of(d):
        return lax.rem(z + d + slabs, slabs)

    def reserve(count):
        used[0] += count
        return used[0] - count

    def remote(src, dst, to, send=None, recv=None):
        if send is None:
            send = recv = reserve(1)
        return pltpu.make_async_remote_copy(
            src_ref=src, dst_ref=dst, send_sem=send_sem.at[send], recv_sem=recv_sem.at[recv],
            device_id=to, device_id_type=MESH,
        )

    def start_all(copies):
        for c in copies:
            c.start()

    def recv_all(copies):
        for c in copies:
            c.wait_recv()

    def sent_all(copies):
        for c in copies:
            c.wait_send()

    loads = [
        pltpu.make_async_copy(ref, inputs.at[i], in_sem.at[i])
        for i, ref in enumerate((vort_hbm, stream_hbm, force_hbm))
    ]
    start_all(loads)
    barrier = pltpu.get_barrier_semaphore()
    peers = [(slot_of(k), z) for k in range(1, SLICES)] + [(t, slab_of(d)) for d in (-3, -2, -1, 1, 2, 3)]
    for p in peers:
        pl.semaphore_signal(barrier, inc=1, device_id=p, device_id_type=MESH)
    for dy in range(3):
        v_in, v_out = conv_in[dy], 0.5 * conv_out[dy]
        for dx in range(3):
            for h in range(8):
                w_in[h, dy * 3 + dx] = jnp.broadcast_to(v_in[dx : dx + 1, h : h + 1], (8, LANES))
                w_out[h, dy * 3 + dx] = jnp.broadcast_to(v_out[dx : dx + 1, h : h + 1], (8, LANES))

    loads[0].wait()
    natural_to_rows(inputs.at[0], nat)
    for c in range(64):
        four = [nat[pl.ds(c * PITCH + q, 8, stride=4), :] for q in range(4)]
        m, k = c // 4, c % 4
        packed[m * 8 : m * 8 + 8, k * LANES : (k + 1) * LANES] = (four[0] + four[1]) + (four[2] + four[3])
    averages = jnp.where(
        lax.broadcasted_iota(jnp.int32, (4 * LANES, LANES), 0) // 4
        == lax.broadcasted_iota(jnp.int32, (4 * LANES, LANES), 1), 0.0625, 0.0,
    ).astype(F32)
    first = jnp.dot(packed[...], averages, precision=HIGH, preferred_element_type=F32)
    spaced_tiles([first[m * 8 : m * 8 + 8] for m in range(BLOCKS)], rolled.at[0])
    mine = pl.ds(2 * t, 3)
    near = [
        remote(rolled.at[0, mine], start.at[:, REACH - 4 - 8 * d : REACH + 4 - 8 * d, :], (t, slab_of(d)))
        for d in (-1, 1, -2, 2, -3, 3)
    ]

    @pl.when(t == 1)
    def _():
        rows_to_chunks(nat, lam)
        store_own(lam, state)

    inside = slice(1, CHUNK + 1)
    halves = [slice(1, 1 + CHUNK // 2), slice(1 + CHUNK // 2, 1 + CHUNK)]
    low, high = slice(OWN - HALO, OWN), slice(OWN + INNER, OWN + INNER + HALO)
    first_rows, last_rows = slice(OWN, OWN + HALO), slice(OWN + INNER - HALO, OWN + INNER)
    sibling = (t + 1 - 2 * parity, z)
    chip = t // 2
    odd = lax.rem(chip, 2) == 1
    across, shared = [], []
    for part in halves:
        across.append(
            [
                remote(fields.at[parity, part, last_rows], fields.at[parity, part, low], (t, slab_of(1))),
                remote(fields.at[parity, part, first_rows], fields.at[parity, part, high], (t, slab_of(-1))),
            ]
        )
        shared.append(
            [remote(fields.at[parity, part, rows], fields.at[parity, part, rows], sibling) for rows in (low, high)]
        )
    helped = [
        remote(fields.at[parity, halves[1], rows], fields.at[parity, halves[1], rows], (slot_of(k), z))
        for rows, k in ((low, SLICES - 2), (high, 2))
    ]
    early = [
        remote(state.at[inside, last_rows], state.at[inside, low], (t, slab_of(1))),
        remote(state.at[inside, first_rows], state.at[inside, high], (t, slab_of(-1))),
    ]
    loads[1].wait()
    loads[2].wait()

    def lay_out(which):
        natural_to_rows(inputs.at[1 + which], nat)
        rows_to_chunks(nat, lam)
        store_own(lam, fields.at[which])

    lay_out(parity)
    pl.semaphore_wait(barrier, len(peers))
    start_all(near)

    @pl.when(jnp.logical_not(odd))
    def _():
        start_all(across[0])

    @pl.when(chip > 0)
    def _():
        start_all(across[1])

    @pl.when(odd)
    def _():
        start_all(across[0])

    @pl.when(t == 1)
    def _():
        start_all(early)

    start[:, REACH - 4 : REACH + 4, :] = rolled[0, mine]
    lay_out(1 - parity)

    recv_all(near)
    win[...] = start[...]
    scratch = (taps, sums, parts)

    def rows_of(ref):
        return lambda r: ref[:, r : r + 8, :]

    def change(a, b):
        return lambda r: a[:, r : r + 8, :] - b[:, r : r + 8, :]

    def deliverer(phase, rows):
        send, recv = reserve(SLICES), reserve(SLICES)
        here = slice(0, rows)

        def copy(n, to, source):
            return remote(
                sent.at[phase, n, :, here], got.at[phase, source, :, here], (to, z), send + n, recv + source
            )

        def put(n, to, read):
            for r in range(0, rows, 8):
                sent[phase, n, :, r : r + 8, :] = own_columns(read(REACH - rows // 2 + r))

            @pl.when(t != to)
            def _():
                copy(n, to, t).start()

            @pl.when(t == to)
            def _():
                got[phase, t, :, here, :] = sent[phase, n, :, here, :]

        def take():
            @pl.when(t > 1)
            def _():
                for k in range(1, SLICES):
                    copy(2, 2, slot_of(k)).wait_recv()

        def done(pairs):
            for n, to in pairs:
                @pl.when(t != to)
                def _():
                    copy(n, to, t).wait_send()

        return put, take, done

    plain = lambda row, count: 0.0
    put_0, take_0, done_0 = deliverer(0, 16)
    for n in range(8):
        coarse_step(-(-(44 - 4 * n) // 8), w_in, w_out, win, old.at[n], plain if n < 7 else None, *scratch)
        if n < 6:
            put_0(n + 1, n + 2, rows_of(win))
        if n == MIDWAY:
            @pl.when(odd)
            def _():
                recv_all(across[1])
                start_all(shared[1])

            @pl.when(chip == 1)
            def _():
                helped[0].start()

            @pl.when(chip == 3)
            def _():
                helped[1].start()

            @pl.when(jnp.logical_not(odd))
            def _():
                recv_all(across[0])
                start_all(shared[0])

    @pl.when(odd)
    def _():
        recv_all(across[0])
        start_all(shared[0])

    @pl.when(jnp.logical_not(odd))
    def _():
        @pl.when(chip == 0)
        def _():
            recv_all(helped)

        @pl.when(chip == 2)
        def _():
            recv_all(across[1])

        start_all(shared[1])

    for part in range(2):
        recv_all(shared[part])
    coefficients(fields.at[0], fields.at[1], pcoef, qcoef, force)
    take_0()

    @pl.when(t == 1)
    def _():
        recv_all(early)
        sent_all(early)

    @pl.when(t > 1)
    def _():
        coarse_in_chunks(got.at[0], coarse)
        spread_coarse(coarse, lambda c, r: None, state)

    @pl.when(t > 0)
    def _():
        ghosts(state)
        fine_run(state, one, two, pcoef, qcoef, force)

    def sharer(phase, shift, wanted, wanted_two):
        place = lax.rem(t + shift, SLICES)
        middle = slice(16, 24)
        send, recv, around = reserve(SLICES), reserve(SLICES), reserve(4 * SLICES)

        def copy(k, slot):
            return remote(
                rolled.at[phase + 1, pl.ds(2 * slot_of(k), 3)], means.at[phase, slot, :, middle],
                (slot_of(k), z), send + k, recv + slot,
            )

        def spread(n):
            return [
                remote(
                    means.at[phase, n, :, middle], means.at[phase, n, :, 16 - 8 * d : 24 - 8 * d],
                    (t, slab_of(d)), around + 4 * n + j, around + 4 * n + j,
                )
                for j, d in enumerate((-1, 1, -2, 2))
                if abs(d) == 1 or n in wanted_two
            ]

        has_slice = functools.reduce(jnp.logical_or, [place == n for n in wanted])

        def go():
            @pl.when(has_slice)
            def _():
                spaced_tiles(block_means(state), rolled.at[phase + 1])
                for k in range(1, SLICES):
                    copy(k, place).start()
                means[phase, place, :, middle, :] = rolled[phase + 1, pl.ds(2 * t, 3)]

        def pass_on():
            for n in wanted:
                @pl.when(place != n)
                def _():
                    copy(1, n).wait_recv()

                start_all(spread(n))

        def take(n):
            recv_all(spread(n))

        def done():
            @pl.when(has_slice)
            def _():
                for k in range(1, SLICES):
                    copy(k, place).wait_send()

            for n in wanted:
                sent_all(spread(n))

        return go, pass_on, take, done

    go_1, pass_1, arrived_1, shared_1 = sharer(0, SLICES - 1, range(0, 7), range(0, 4))
    go_1()
    copy_f = remote(state.at[inside, slice(OWN, OWN + INNER)], one.at[inside, slice(OWN, OWN + INNER)], (0, z))

    @pl.when(t == 1)
    def _():
        copy_f.start()

    bulk = [
        remote(state.at[1 + a : 1 + b, rows], edge.at[side, a:b], (t, slab_of(1 - 2 * side)))
        for a, b in ((0, AHEAD), (AHEAD, CHUNK))
        for side, rows in enumerate((last_rows, first_rows))
    ]

    @pl.when(t > 0)
    def _():
        start_all(bulk[:2])

    pass_1()

    @pl.when(t > 0)
    def _():
        start_all(bulk[2:])

    def corrected(phase, n, before):
        def extra(row, count):
            there = pl.ds(row - 8, 8, stride=count)
            return means[phase, n, :, there, :] - before[n, :, pl.ds(row, 8, stride=count), :]

        return extra

    put_1, take_1, done_1 = deliverer(1, 16)
    arrived_1(0)
    win[:, 8:48, :] = means[0, 0]
    for n in range(1, 8):
        if n < 7:
            arrived_1(n)
        coarse_step(
            -(-(44 - 4 * n) // 8), w_in, w_out, win, new.at[n], corrected(0, n, old) if n < 7 else None, *scratch
        )
        if n < 7:
            put_1(n, n + 1, change(new.at[n], old.at[n]))

    take_1()

    @pl.when(t == 1)
    def _():
        copy_f.wait_send()
        got[1] = jnp.zeros(got.shape[1:], F32)

    @pl.when(t > 0)
    def _():
        recv_all(bulk)
        sent_all(bulk)
        coarse_in_chunks(got.at[1], coarse)

        def base(c, r):
            if r < 2:
                return edge[0, c, 8 * r : 8 * r + 8, :]
            if r >= 6:
                return edge[1, c, 8 * (r - 6) : 8 * (r - 6) + 8, :]
            return state[pl.ds(c.start + 1, 4), PAD + 8 * r : PAD + 8 * r + 8, :]

        spread_coarse(coarse, base, state)
        ghosts(state)
        fine_run(state, one, two, pcoef, qcoef, force)

    go_2, pass_2, arrived_2, shared_2 = sharer(1, 0, range(1, 7), range(1, 3))
    go_2()
    pass_2()

    @pl.when(t == 0)
    def _():
        copy_f.wait_recv()
        load_own(one, lam)

    @pl.when(t > 0)
    def _():
        load_own(state, lam)

    put_2, take_2, done_2 = deliverer(2, 8)
    arrived_2(1)
    win[:, 8:48, :] = means[1, 1]
    for n in range(2, 8):
        if n < 7:
            arrived_2(n)
        coarse_step(
            -(-(40 - 4 * n) // 8), w_in, w_out, win, old.at[n], corrected(1, n, new) if n < 7 else None, *scratch
        )
        put_2(n, n, change(old.at[n], new.at[n]))

    chunks_to_rows(lam, nat)
    for c in range(64):
        out[:, c * LANES : (c + 1) * LANES] = nat[c * PITCH : c * PITCH + INNER, :]

    @pl.when(t <= 1)
    def _():
        got[2] = jnp.zeros(got.shape[1:], F32)

    sent_all(near)
    sent_all(across[0])

    @pl.when(chip > 0)
    def _():
        sent_all(across[1])

    @pl.when(chip == 1)
    def _():
        helped[0].wait_send()

    @pl.when(chip == 3)
    def _():
        helped[1].wait_send()

    for part in range(2):
        sent_all(shared[part])
    done_0([(n, n + 1) for n in range(1, 7)])
    done_1([(n, n + 1) for n in range(1, 7)])
    done_2([(n, n) for n in range(2, 8)])
    shared_1()
    shared_2()
    take_2()
    for m in range(BLOCKS):
        delta_out[m * 8 : m * 8 + 8, :] = got[2, m // 2, m % 2, 0:8, :]


def finish_kernel(fine, delta, out):
    copies = jnp.where(
        lax.broadcasted_iota(jnp.int32, (LANES, 4 * LANES), 0)
        == lax.broadcasted_iota(jnp.int32, (LANES, 4 * LANES), 1) // 4, 1.0, 0.0,
    ).astype(F32)
    wide = jnp.dot(delta[...], copies, precision=HIGH, preferred_element_type=F32)
    upper = lax.broadcasted_iota(jnp.int32, (8, 4 * LANES), 0) < 4
    for m in range(delta.shape[0] // 8):
        cols = slice(m * 4 * LANES, (m + 1) * 4 * LANES)
        for a in range(INNER // 8):
            r = m * 8 + 2 * a
            v = jnp.where(upper, wide[r : r + 1], wide[r + 1 : r + 2])
            out[0, a * 8 : a * 8 + 8, cols] = fine[a * 8 : a * 8 + 8, cols] + v


def body(vorticity, stream, forcing, conv_in, conv_out):
    rows, cols = vorticity.shape
    whole = (CHUNK + 2, TALL, LANES)
    vmem = pl.BlockSpec(memory_space=VMEM)
    anywhere = pl.BlockSpec(memory_space=pl.ANY)
    window = (3, WINDOW, LANES)
    shapes = [
        (3, rows, cols), (64 * PITCH, LANES), (CHUNK * PITCH, LANES), (2,) + whole, whole, whole, whole, whole, whole,
        (4,) + whole, window, window, (SLICES,) + window, (SLICES,) + window,
        (9, 18, 8, LANES), (9, 18, 8, LANES), (3, 8, 3, 8, LANES), (8, 9, 8, LANES), (8, 9, 8, LANES),
        (3, BLOCKS + 2, 8, LANES), (2, SLICES, 3, 40, LANES), (3, SLICES, 2, 16, LANES), (3, SLICES, 2, 16, LANES),
        (2, CHUNK, HALO, LANES), (BLOCKS, 16, LANES), (8 * BLOCKS, 4 * LANES),
    ]
    slots = 176
    fine, delta = pl.pallas_call(
        kernel,
        name="parareal",
        out_shape=(jax.ShapeDtypeStruct((rows, cols), F32), jax.ShapeDtypeStruct((8 * BLOCKS, LANES), F32)),
        in_specs=[vmem, vmem, anywhere, anywhere, anywhere],
        out_specs=(vmem, vmem),
        scratch_shapes=[VMEM(s, F32) for s in shapes]
        + [pltpu.SemaphoreType.DMA((3,)), pltpu.SemaphoreType.DMA((slots,)), pltpu.SemaphoreType.DMA((slots,))],
        compiler_params=pltpu.CompilerParams(vmem_limit_bytes=62 * 2**20, collective_id=0, has_side_effects=True),
    )(jnp.transpose(conv_in, (1, 2, 0)), jnp.transpose(conv_out, (1, 2, 0)), vorticity, stream, forcing)
    grid = 2
    return pl.pallas_call(
        finish_kernel,
        name="finish",
        grid=(grid,),
        out_shape=jax.ShapeDtypeStruct((1, rows, cols), F32),
        in_specs=[
            pl.BlockSpec((rows, cols // grid), lambda i: (0, i)),
            pl.BlockSpec((8 * BLOCKS // grid, LANES), lambda i: (i, 0)),
        ],
        out_specs=pl.BlockSpec((1, rows, cols // grid), lambda i: (0, 0, i)),
    )(fine, delta)


def solution(mesh):
    placed = (P("space", None), P("space", None), P("space", None), P(), P())
    return jax.shard_map(
        body, mesh=mesh, in_specs=placed, out_specs=P("tm", "space", None), check_vma=False
    )
```

```python
import functools
import math

import jax
import jax.numpy as jnp
import numpy as np
from jax import lax
from jax.experimental import pallas as pl
from jax.experimental.pallas import tpu as pltpu
from jax.sharding import PartitionSpec as P

F32 = jnp.float32
VMEM = pltpu.VMEM
MESH = pl.DeviceIdType.MESH
HIGH = lax.Precision.HIGHEST

STEPS = 4
SLICES = 8
LANES = 128
CHUNK = 64
INNER = 32
HALO = 16
PAD = 8
TALL = INNER + 2 * HALO + 2 * PAD
OWN = PAD + HALO
PITCH = 33
BLOCKS = 16
REACH = 28
WINDOW = 2 * REACH


def fine_weights():
    shift = np.polynomial.Polynomial([-0.45, 0.2])
    of_w = sum(shift**j / math.factorial(j) for j in range(5))
    of_f = sum(shift**j / math.factorial(j + 1) for j in range(4))
    return [float(v) for v in of_w.coef], [float(v) for v in of_f.coef] + [0.0]


def lane_iota():
    return lax.broadcasted_iota(jnp.int32, (8, LANES), 1)


def lane_shifted(value, up):
    lane = lax.broadcasted_iota(jnp.int32, value.shape, 2)
    if up:
        rolled = pltpu.roll(value, LANES - 1, 2)
        return jnp.where(lane == LANES - 1, jnp.concatenate([rolled[1:], rolled[:1]], axis=0), rolled)
    rolled = pltpu.roll(value, 1, 2)
    return jnp.where(lane == 0, jnp.concatenate([rolled[-1:], rolled[:-1]], axis=0), rolled)


def lane_gather(value, index):
    return jnp.take_along_axis(value, index, axis=1)


def next_chunk():
    lane = lane_iota()
    return jnp.where(lane < 64, lane + 64, jnp.where(lane == 127, 0, lane - 63))


def previous_chunk():
    lane = lane_iota()
    return jnp.where(lane >= 64, lane - 64, jnp.where(lane == 0, 127, lane + 63))


def swap_tiles_and_lanes(tiles):
    lane = lane_iota()
    for bit in range(4):
        width = 4 << bit
        high = (lane // width) % 2 == 1
        out = list(tiles)
        for m in range(16):
            if not m >> bit & 1:
                a, b = tiles[m], tiles[m | 1 << bit]
                out[m] = jnp.where(high, pltpu.roll(b, width, 1), a)
                out[m | 1 << bit] = jnp.where(high, b, pltpu.roll(a, LANES - width, 1))
        tiles = out
    return tiles


def to_chunks(tiles):
    lane = lane_iota()
    index = ((lane % 4) * 2 + lane // 64) * 16 + (lane % 64) // 4
    return swap_tiles_and_lanes([lane_gather(t, index) for t in tiles])


def from_chunks(tiles):
    lane = lane_iota()
    block = lane // 16
    index = (block % 2) * 64 + (lane % 16) * 4 + block // 2
    return [lane_gather(t, index) for t in swap_tiles_and_lanes(tiles)]


def coarse_step(count, w_in, w_out, win, values, extra, taps, sums, parts):
    lanes = win.shape[0]
    off = REACH - 4 * count
    at = [pl.ds(off + q, 8, stride=count) for q in range(count)]

    def tiles(q):
        return slice(lanes * q, lanes * q + lanes)

    for q in range(count):
        x = win[:, at[q], :]
        for dx, v in enumerate((lane_shifted(x, False), x, lane_shifted(x, True))):
            for dy in range(3):
                place = q + 1 - dy
                if place < 0:
                    taps[dy * 3 + dx, tiles(count - 1)] = pltpu.roll(v, 7, 1)
                elif place >= count:
                    taps[dy * 3 + dx, tiles(0)] = pltpu.roll(v, 1, 1)
                else:
                    taps[dy * 3 + dx, tiles(place)] = v
    total = lanes * count
    group = GROUP

    def few(i, _):
        some = pl.ds(jnp.minimum(i * group, total - group), group)
        x = taps[:, some]
        acc = None
        for h in range(8):
            hidden = jnp.tanh(jnp.sum(w_in[h][:, None] * x, axis=0))
            term = w_out[h][:, None] * hidden[None]
            acc = term if acc is None else acc + term
        sums[:, some] = acc
        return 0

    lax.fori_loop(0, -(-total // group), few, 0)
    for q in range(count):
        for dy in range(3):
            low = lane_shifted(sums[dy * 3, tiles(q)], False)
            high = lane_shifted(sums[dy * 3 + 2, tiles(q)], True)
            v = low + high + sums[dy * 3 + 1, tiles(q)]
            parts[dy, q + 1] = v
            if q == 0 and dy == 2:
                parts[dy, count + 1] = pltpu.roll(v, 7, 1)
            if q == count - 1 and dy == 0:
                parts[dy, 0] = pltpu.roll(v, 1, 1)
    for q in range(count):
        g = win[:, at[q], :] + (parts[0, q] + parts[1, q + 1] + parts[2, q + 2])
        values[:, at[q], :] = g
        if extra is not None:
            win[:, at[q], :] = g + extra(off + q, count)


def own_columns(value):
    rolled = pltpu.roll(value, 64, 2)
    lane = lax.broadcasted_iota(jnp.int32, (2, 8, LANES), 2)
    return jnp.where(lane < 64, rolled[:2], rolled[1:])


def fine_stage(src, dst, base, pcoef, qcoef, force, off, count, scale, of_base):
    at = [pl.ds(off + q, 8, stride=count) for q in range(-1, count + 1)]

    def block(first, size):
        centre = pl.ds(first, size)
        wide = [src[pl.ds(first - 1, size + 2), a, :] for a in at[1:-1]]
        column = [src[centre, at[0], :]] + [x[1:-1] for x in wide] + [src[centre, at[-1], :]]
        results = []
        for q in range(count):
            slot = (centre, at[q + 1], slice(None))
            left, right = wide[q][:-2], wide[q][2:]
            above, below = column[q + 2], column[q]
            t = pcoef[slot] * (right - left) + qcoef[slot] * (above - below) + (left + below)
            if scale != 1.0:
                t = scale * t
            here = column[q + 1] if src is base else base[slot]
            t = t + (of_base * here + force[slot])
            dst[slot] = t
            results.append(t)
        return results

    group = 10
    last = block(CHUNK - 1, 2)
    first = block(1, 2)
    block(3, group)
    ahead, back = next_chunk(), previous_chunk()
    for q in range(count):
        dst[0, at[q + 1], :] = lane_gather(last[q][1], back)
        dst[CHUNK + 1, at[q + 1], :] = lane_gather(first[q][0], ahead)

    def body(g, _):
        block(3 + g * group, group)
        return 0

    lax.fori_loop(1, (CHUNK - 4) // group, body, 0)


def fine_run(state, one, two, pcoef, qcoef, force):
    of_w, _ = fine_weights()
    for step in range(STEPS):
        count = 9 if step == 0 else 8 - step
        off = 4 if step == 0 else PAD + 4 * step
        shared = (state, pcoef, qcoef)
        fine_stage(state, one, *shared, force.at[3], off, count, 1.0, of_w[3] / of_w[4])
        fine_stage(one, two, *shared, force.at[2], off, count, 1.0, of_w[2] / of_w[4])
        fine_stage(two, one, *shared, force.at[1], off, count, 1.0, of_w[1] / of_w[4])
        fine_stage(one, state, *shared, force.at[0], off, count, of_w[4], of_w[0])


def ghosts(ref):
    ahead, back = next_chunk(), previous_chunk()
    for r in range(PAD, TALL - PAD, 8):
        ref[0, r : r + 8, :] = lane_gather(ref[CHUNK, r : r + 8, :], back)
        ref[CHUNK + 1, r : r + 8, :] = lane_gather(ref[1, r : r + 8, :], ahead)


def coefficients(stream, forcing, pcoef, qcoef, force):
    of_w, of_f = fine_weights()
    ghosts(stream)
    count = 9
    at = [pl.ds(4 + q, 8, stride=count) for q in range(-1, count + 1)]

    group = 4

    def body(g, _):
        first = 1 + g * group
        c = pl.ds(first, group)
        wide = [stream[pl.ds(first - 1, group + 2), a, :] for a in at[1:-1]]
        x = [stream[c, at[0], :]] + [v[1:-1] for v in wide] + [stream[c, at[-1], :]]
        for q in range(count):
            a = at[q + 1]
            pcoef[c, a, :] = 0.5 - 1.25 * (x[q + 2] - x[q])
            qcoef[c, a, :] = 0.5 + 1.25 * (wide[q][2:] - wide[q][:-2])
            f = forcing[c, a, :]
            force[0, c, a, :] = of_f[0] * f
            for k in range(1, 4):
                force[k, c, a, :] = (of_f[k] / of_w[4]) * f
        return 0

    lax.fori_loop(0, CHUNK // group, body, 0)


def natural_to_rows(source, nat):
    for c in range(64):
        nat[c * PITCH : c * PITCH + INNER, :] = source[:, c * LANES : (c + 1) * LANES]


def rows_to_chunks(nat, lam):
    low = lax.broadcasted_iota(jnp.int32, (64, LANES), 1) < 64
    for i in range(INNER // 2):
        j = i + INNER // 2
        at_i, at_j = pl.ds(i, 64, stride=PITCH), pl.ds(j, 64, stride=PITCH)
        flipped = jnp.concatenate([nat[at_i, :], nat[at_j, :]], axis=0).T
        top, bottom = flipped[:64], flipped[64:]
        lam[at_i, :] = jnp.where(low, top, pltpu.roll(bottom, 64, 1))
        lam[at_j, :] = jnp.where(low, pltpu.roll(top, 64, 1), bottom)


def chunks_to_rows(lam, nat):
    low = lax.broadcasted_iota(jnp.int32, (64, LANES), 1) < 64
    for i in range(INNER // 2):
        j = i + INNER // 2
        at_i, at_j = pl.ds(i, 64, stride=PITCH), pl.ds(j, 64, stride=PITCH)
        x, y = lam[at_i, :], lam[at_j, :]
        top = jnp.where(low, x, pltpu.roll(y, 64, 1))
        bottom = jnp.where(low, pltpu.roll(x, 64, 1), y)
        flipped = jnp.concatenate([top, bottom], axis=0).T
        nat[at_i, :] = flipped[:64]
        nat[at_j, :] = flipped[64:]


def store_own(lam, ref):
    for c in range(CHUNK):
        ref[1 + c, OWN : OWN + INNER, :] = lam[c * PITCH : c * PITCH + INNER, :]


def load_own(ref, lam):
    for c in range(CHUNK):
        lam[c * PITCH : c * PITCH + INNER, :] = ref[1 + c, OWN : OWN + INNER, :]


def spaced_tiles(tiles, rolled):
    lane = lane_iota()
    turned = [pltpu.roll(t, 64, 1) for t in tiles]
    for k in range(BLOCKS):
        v = jnp.where(lane < 64, turned[k - 1], turned[k])
        rolled[k] = v
        if k < 2:
            rolled[BLOCKS + k] = v


def block_means(state):
    tiles = []
    for m in range(BLOCKS):
        four = [state[1 + 4 * m : 5 + 4 * m, pl.ds(OWN + q, 8, stride=4), :] for q in range(4)]
        tiles.append(0.0625 * jnp.sum((four[0] + four[1]) + (four[2] + four[3]), axis=0))
    return from_chunks(tiles)


def coarse_in_chunks(pieces, coarse):
    for half in range(2):
        at = pl.ds(half, 8, stride=2)
        tiles = to_chunks([pieces[m // 2, m % 2, at, :] for m in range(BLOCKS)])
        for m in range(BLOCKS):
            coarse[m, at, :] = tiles[m]


def spread_coarse(coarse, base, state):
    upper = lax.broadcasted_iota(jnp.int32, (8, LANES), 0) < 4

    def body(m, _):
        c = pl.ds(4 * m, 4)
        for r in range(8):
            v = jnp.where(upper, coarse[m, 2 * r : 2 * r + 1, :], coarse[m, 2 * r + 1 : 2 * r + 2, :])[None]
            old = base(c, r)
            v = jnp.broadcast_to(v, (4, 8, LANES)) if old is None else old + v
            state[pl.ds(4 * m + 1, 4), PAD + 8 * r : PAD + 8 * r + 8, :] = v
        return 0

    lax.fori_loop(0, BLOCKS, body, 0)


GROUP = 3
AHEAD = 24
FIRST_PART, SECOND_PART = 0, 4


def kernel(
    conv_in, conv_out, vort_hbm, stream_hbm, force_hbm, out, delta_out,
    inputs, nat, lam, fields, state, one, two, pcoef, qcoef, force,
    start, win, old, new, taps, sums, parts, w_in, w_out,
    rolled, means, sent, got, edge, coarse, packed,
    in_sem, send_sem, recv_sem,
):
    t, z = lax.axis_index("tm"), lax.axis_index("space")
    slabs = lax.axis_size("space")
    parity = lax.rem(t, 2)
    used = [0]

    def slot_of(k):
        return lax.rem(t + k, SLICES)

    def slab_of(d):
        return lax.rem(z + d + slabs, slabs)

    def reserve(count):
        used[0] += count
        return used[0] - count

    def remote(src, dst, to, send=None, recv=None):
        if send is None:
            send = recv = reserve(1)
        return pltpu.make_async_remote_copy(
            src_ref=src, dst_ref=dst, send_sem=send_sem.at[send], recv_sem=recv_sem.at[recv],
            device_id=to, device_id_type=MESH,
        )

    def start_all(copies):
        for c in copies:
            c.start()

    def recv_all(copies):
        for c in copies:
            c.wait_recv()

    def sent_all(copies):
        for c in copies:
            c.wait_send()

    loads = [
        pltpu.make_async_copy(ref, inputs.at[i], in_sem.at[i])
        for i, ref in enumerate((vort_hbm, stream_hbm, force_hbm))
    ]
    start_all(loads)
    barrier = pltpu.get_barrier_semaphore()
    peers = [(slot_of(k), z) for k in range(1, SLICES)] + [(t, slab_of(d)) for d in (-3, -2, -1, 1, 2, 3)]
    for p in peers:
        pl.semaphore_signal(barrier, inc=1, device_id=p, device_id_type=MESH)
    for dy in range(3):
        v_in, v_out = conv_in[dy], 0.5 * conv_out[dy]
        for dx in range(3):
            for h in range(8):
                w_in[h, dy * 3 + dx] = jnp.broadcast_to(v_in[dx : dx + 1, h : h + 1], (8, LANES))
                w_out[h, dy * 3 + dx] = jnp.broadcast_to(v_out[dx : dx + 1, h : h + 1], (8, LANES))

    loads[0].wait()
    natural_to_rows(inputs.at[0], nat)
    for c in range(64):
        four = [nat[pl.ds(c * PITCH + q, 8, stride=4), :] for q in range(4)]
        m, k = c // 4, c % 4
        packed[m * 8 : m * 8 + 8, k * LANES : (k + 1) * LANES] = (four[0] + four[1]) + (four[2] + four[3])
    averages = jnp.where(
        lax.broadcasted_iota(jnp.int32, (4 * LANES, LANES), 0) // 4
        == lax.broadcasted_iota(jnp.int32, (4 * LANES, LANES), 1), 0.0625, 0.0,
    ).astype(F32)
    first = jnp.dot(packed[...], averages, precision=HIGH, preferred_element_type=F32)
    spaced_tiles([first[m * 8 : m * 8 + 8] for m in range(BLOCKS)], rolled.at[0])
    mine = pl.ds(2 * t, 3)
    near = [
        remote(rolled.at[0, mine], start.at[:, REACH - 4 - 8 * d : REACH + 4 - 8 * d, :], (t, slab_of(d)))
        for d in (-1, 1, -2, 2, -3, 3)
    ]

    @pl.when(t == 1)
    def _():
        rows_to_chunks(nat, lam)
        store_own(lam, state)

    inside = slice(1, CHUNK + 1)
    low, high = slice(OWN - HALO, OWN), slice(OWN + INNER, OWN + INNER + HALO)
    first_rows, last_rows = slice(OWN, OWN + HALO), slice(OWN + INNER - HALO, OWN + INNER)
    sibling = (t + 1 - 2 * parity, z)
    half = lax.rem(t // 2, 2)
    size = CHUNK // 4

    def part_of(which, part):
        return pl.ds(1 + 2 * size * which + size * part, size)

    across, helped, shared = [], [], [[], []]
    for part in range(2):
        some = part_of(half, part)
        across.append(
            [
                remote(fields.at[parity, some, last_rows], fields.at[parity, some, low], (t, slab_of(1))),
                remote(fields.at[parity, some, first_rows], fields.at[parity, some, high], (t, slab_of(-1))),
            ]
        )
        helped.append(
            [
                remote(fields.at[parity, some, rows], fields.at[parity, some, rows], (slot_of(k), z))
                for rows, k in ((low, SLICES - 2), (high, 2))
            ]
        )
        for k, which in enumerate((half, 1 - half)):
            some = part_of(which, part)
            shared[k].append(
                [remote(fields.at[parity, some, rows], fields.at[parity, some, rows], sibling) for rows in (low, high)]
            )
    early = [
        remote(state.at[inside, last_rows], state.at[inside, low], (t, slab_of(1))),
        remote(state.at[inside, first_rows], state.at[inside, high], (t, slab_of(-1))),
    ]
    loads[1].wait()
    loads[2].wait()

    def lay_out(which):
        natural_to_rows(inputs.at[1 + which], nat)
        rows_to_chunks(nat, lam)
        store_own(lam, fields.at[which])

    lay_out(parity)
    pl.semaphore_wait(barrier, len(peers))
    start_all(near)

    start_all(across[0])
    start_all(across[1])

    @pl.when(t == 1)
    def _():
        start_all(early)

    start[:, REACH - 4 : REACH + 4, :] = rolled[0, mine]
    lay_out(1 - parity)

    recv_all(near)
    win[...] = start[...]
    scratch = (taps, sums, parts)

    def rows_of(ref):
        return lambda r: ref[:, r : r + 8, :]

    def change(a, b):
        return lambda r: a[:, r : r + 8, :] - b[:, r : r + 8, :]

    def deliverer(phase, rows):
        send, recv = reserve(SLICES), reserve(SLICES)
        here = slice(0, rows)

        def copy(n, to, source):
            return remote(
                sent.at[phase, n, :, here], got.at[phase, source, :, here], (to, z), send + n, recv + source
            )

        def put(n, to, read):
            for r in range(0, rows, 8):
                sent[phase, n, :, r : r + 8, :] = own_columns(read(REACH - rows // 2 + r))

            @pl.when(t != to)
            def _():
                copy(n, to, t).start()

            @pl.when(t == to)
            def _():
                got[phase, t, :, here, :] = sent[phase, n, :, here, :]

        def take():
            @pl.when(t > 1)
            def _():
                for k in range(1, SLICES):
                    copy(2, 2, slot_of(k)).wait_recv()

        def done(pairs):
            for n, to in pairs:
                @pl.when(t != to)
                def _():
                    copy(n, to, t).wait_send()

        return put, take, done

    plain = lambda row, count: 0.0
    put_0, take_0, done_0 = deliverer(0, 16)
    for n in range(8):
        coarse_step(-(-(44 - 4 * n) // 8), w_in, w_out, win, old.at[n], plain if n < 7 else None, *scratch)
        if n < 6:
            put_0(n + 1, n + 2, rows_of(win))
        if n == FIRST_PART or n == SECOND_PART:
            part = int(n == SECOND_PART)
            recv_all(across[part])
            start_all(helped[part])
            start_all(shared[0][part])
        if n >= 6:
            recv_all(helped[n - 6])
            start_all(shared[1][n - 6])

    take_0()

    @pl.when(t > 1)
    def _():
        coarse_in_chunks(got.at[0], coarse)
        spread_coarse(coarse, lambda c, r: None, state)

    for copies in shared:
        for part in range(2):
            recv_all(copies[part])
    coefficients(fields.at[0], fields.at[1], pcoef, qcoef, force)

    @pl.when(t == 1)
    def _():
        recv_all(early)
        sent_all(early)

    @pl.when(t > 0)
    def _():
        ghosts(state)
        fine_run(state, one, two, pcoef, qcoef, force)

    def sharer(phase, shift, wanted, wanted_two):
        place = lax.rem(t + shift, SLICES)
        middle = slice(16, 24)
        send, recv, around = reserve(SLICES), reserve(SLICES), reserve(4 * SLICES)

        def copy(k, slot):
            return remote(
                rolled.at[phase + 1, pl.ds(2 * slot_of(k), 3)], means.at[phase, slot, :, middle],
                (slot_of(k), z), send + k, recv + slot,
            )

        def spread(n):
            return [
                remote(
                    means.at[phase, n, :, middle], means.at[phase, n, :, 16 - 8 * d : 24 - 8 * d],
                    (t, slab_of(d)), around + 4 * n + j, around + 4 * n + j,
                )
                for j, d in enumerate((-1, 1, -2, 2))
                if abs(d) == 1 or n in wanted_two
            ]

        has_slice = functools.reduce(jnp.logical_or, [place == n for n in wanted])

        def go():
            @pl.when(has_slice)
            def _():
                spaced_tiles(block_means(state), rolled.at[phase + 1])
                for k in range(1, SLICES):
                    copy(k, place).start()
                means[phase, place, :, middle, :] = rolled[phase + 1, pl.ds(2 * t, 3)]

        def pass_on():
            for n in wanted:
                @pl.when(place != n)
                def _():
                    copy(1, n).wait_recv()

                start_all(spread(n))

        def take(n):
            recv_all(spread(n))

        def done():
            @pl.when(has_slice)
            def _():
                for k in range(1, SLICES):
                    copy(k, place).wait_send()

            for n in wanted:
                sent_all(spread(n))

        return go, pass_on, take, done

    go_1, pass_1, arrived_1, shared_1 = sharer(0, SLICES - 1, range(0, 7), range(0, 4))
    go_1()
    copy_f = remote(state.at[inside, slice(OWN, OWN + INNER)], one.at[inside, slice(OWN, OWN + INNER)], (0, z))

    @pl.when(t == 1)
    def _():
        copy_f.start()

    bulk = [
        remote(state.at[1 + a : 1 + b, rows], edge.at[side, a:b], (t, slab_of(1 - 2 * side)))
        for a, b in ((0, AHEAD), (AHEAD, CHUNK))
        for side, rows in enumerate((last_rows, first_rows))
    ]

    @pl.when(t > 0)
    def _():
        start_all(bulk[:2])

    pass_1()

    @pl.when(t > 0)
    def _():
        start_all(bulk[2:])

    def corrected(phase, n, before):
        def extra(row, count):
            there = pl.ds(row - 8, 8, stride=count)
            return means[phase, n, :, there, :] - before[n, :, pl.ds(row, 8, stride=count), :]

        return extra

    put_1, take_1, done_1 = deliverer(1, 16)
    arrived_1(0)
    win[:, 8:48, :] = means[0, 0]
    for n in range(1, 8):
        if n < 7:
            arrived_1(n)
        coarse_step(
            -(-(44 - 4 * n) // 8), w_in, w_out, win, new.at[n], corrected(0, n, old) if n < 7 else None, *scratch
        )
        if n < 7:
            put_1(n, n + 1, change(new.at[n], old.at[n]))

    take_1()

    @pl.when(t == 1)
    def _():
        copy_f.wait_send()
        got[1] = jnp.zeros(got.shape[1:], F32)

    @pl.when(t > 0)
    def _():
        recv_all(bulk)
        sent_all(bulk)
        coarse_in_chunks(got.at[1], coarse)

        def base(c, r):
            if r < 2:
                return edge[0, c, 8 * r : 8 * r + 8, :]
            if r >= 6:
                return edge[1, c, 8 * (r - 6) : 8 * (r - 6) + 8, :]
            return state[pl.ds(c.start + 1, 4), PAD + 8 * r : PAD + 8 * r + 8, :]

        spread_coarse(coarse, base, state)
        ghosts(state)
        fine_run(state, one, two, pcoef, qcoef, force)

    go_2, pass_2, arrived_2, shared_2 = sharer(1, 0, range(1, 7), range(1, 3))
    go_2()
    pass_2()

    @pl.when(t == 0)
    def _():
        copy_f.wait_recv()
        load_own(one, lam)

    @pl.when(t > 0)
    def _():
        load_own(state, lam)

    put_2, take_2, done_2 = deliverer(2, 8)
    arrived_2(1)
    win[:, 8:48, :] = means[1, 1]
    for n in range(2, 8):
        if n < 7:
            arrived_2(n)
        coarse_step(
            -(-(40 - 4 * n) // 8), w_in, w_out, win, old.at[n], corrected(1, n, new) if n < 7 else None, *scratch
        )
        put_2(n, n, change(old.at[n], new.at[n]))

    chunks_to_rows(lam, nat)
    for c in range(64):
        inputs[0, :, c * LANES : (c + 1) * LANES] = nat[c * PITCH : c * PITCH + INNER, :]
    store = pltpu.make_async_copy(inputs.at[0], out, in_sem.at[0])
    store.start()

    @pl.when(t <= 1)
    def _():
        got[2] = jnp.zeros(got.shape[1:], F32)

    sent_all(near)
    for part in range(2):
        sent_all(across[part])
        sent_all(helped[part])
        sent_all(shared[0][part])
        sent_all(shared[1][part])
    done_0([(n, n + 1) for n in range(1, 7)])
    done_1([(n, n + 1) for n in range(1, 7)])
    done_2([(n, n) for n in range(2, 8)])
    shared_1()
    shared_2()
    take_2()
    for m in range(BLOCKS):
        delta_out[m * 8 : m * 8 + 8, :] = got[2, m // 2, m % 2, 0:8, :]
    store.wait()


def finish_kernel(fine, delta, out):
    copies = jnp.where(
        lax.broadcasted_iota(jnp.int32, (LANES, 4 * LANES), 0)
        == lax.broadcasted_iota(jnp.int32, (LANES, 4 * LANES), 1) // 4, 1.0, 0.0,
    ).astype(F32)
    wide = jnp.dot(delta[...], copies, precision=HIGH, preferred_element_type=F32)
    upper = lax.broadcasted_iota(jnp.int32, (8, 4 * LANES), 0) < 4
    for m in range(delta.shape[0] // 8):
        cols = slice(m * 4 * LANES, (m + 1) * 4 * LANES)
        for a in range(INNER // 8):
            r = m * 8 + 2 * a
            v = jnp.where(upper, wide[r : r + 1], wide[r + 1 : r + 2])
            out[0, a * 8 : a * 8 + 8, cols] = fine[a * 8 : a * 8 + 8, cols] + v


def body(vorticity, stream, forcing, conv_in, conv_out):
    rows, cols = vorticity.shape
    whole = (CHUNK + 2, TALL, LANES)
    vmem = pl.BlockSpec(memory_space=VMEM)
    anywhere = pl.BlockSpec(memory_space=pl.ANY)
    window = (3, WINDOW, LANES)
    shapes = [
        (3, rows, cols), (64 * PITCH, LANES), (CHUNK * PITCH, LANES), (2,) + whole, whole, whole, whole, whole, whole,
        (4,) + whole, window, window, (SLICES,) + window, (SLICES,) + window,
        (9, 18, 8, LANES), (9, 18, 8, LANES), (3, 8, 3, 8, LANES), (8, 9, 8, LANES), (8, 9, 8, LANES),
        (3, BLOCKS + 2, 8, LANES), (2, SLICES, 3, 40, LANES), (3, SLICES, 2, 16, LANES), (3, SLICES, 2, 16, LANES),
        (2, CHUNK, HALO, LANES), (BLOCKS, 16, LANES), (8 * BLOCKS, 4 * LANES),
    ]
    slots = 176
    fine, delta = pl.pallas_call(
        kernel,
        name="parareal",
        out_shape=(jax.ShapeDtypeStruct((rows, cols), F32), jax.ShapeDtypeStruct((8 * BLOCKS, LANES), F32)),
        in_specs=[vmem, vmem, anywhere, anywhere, anywhere],
        out_specs=(anywhere, vmem),
        scratch_shapes=[VMEM(s, F32) for s in shapes]
        + [pltpu.SemaphoreType.DMA((3,)), pltpu.SemaphoreType.DMA((slots,)), pltpu.SemaphoreType.DMA((slots,))],
        compiler_params=pltpu.CompilerParams(vmem_limit_bytes=62 * 2**20, collective_id=0, has_side_effects=True),
    )(jnp.transpose(conv_in, (1, 2, 0)), jnp.transpose(conv_out, (1, 2, 0)), vorticity, stream, forcing)
    grid = 2
    return pl.pallas_call(
        finish_kernel,
        name="finish",
        grid=(grid,),
        out_shape=jax.ShapeDtypeStruct((1, rows, cols), F32),
        in_specs=[
            pl.BlockSpec((rows, cols // grid), lambda i: (0, i)),
            pl.BlockSpec((8 * BLOCKS // grid, LANES), lambda i: (i, 0)),
        ],
        out_specs=pl.BlockSpec((1, rows, cols // grid), lambda i: (0, 0, i)),
    )(fine, delta)


def solution(mesh):
    placed = (P("space", None), P("space", None), P("space", None), P(), P())
    return jax.shard_map(
        body, mesh=mesh, in_specs=placed, out_specs=P("tm", "space", None), check_vma=False
    )
```

```python
import functools
import math

import jax
import jax.numpy as jnp
import numpy as np
from jax import lax
from jax.experimental import pallas as pl
from jax.experimental.pallas import tpu as pltpu
from jax.sharding import PartitionSpec as P

F32 = jnp.float32
VMEM = pltpu.VMEM
MESH = pl.DeviceIdType.MESH
HIGH = lax.Precision.HIGHEST

STEPS = 4
SLICES = 8
LANES = 128
CHUNK = 64
INNER = 32
HALO = 16
PAD = 8
TALL = INNER + 2 * HALO + 2 * PAD
OWN = PAD + HALO
PITCH = 33
BLOCKS = 16
REACH = 28
WINDOW = 2 * REACH


def fine_weights():
    shift = np.polynomial.Polynomial([-0.45, 0.2])
    of_w = sum(shift**j / math.factorial(j) for j in range(5))
    of_f = sum(shift**j / math.factorial(j + 1) for j in range(4))
    return [float(v) for v in of_w.coef], [float(v) for v in of_f.coef] + [0.0]


def lane_iota():
    return lax.broadcasted_iota(jnp.int32, (8, LANES), 1)


def lane_shifted(value, up):
    lane = lax.broadcasted_iota(jnp.int32, value.shape, 2)
    if up:
        rolled = pltpu.roll(value, LANES - 1, 2)
        return jnp.where(lane == LANES - 1, jnp.concatenate([rolled[1:], rolled[:1]], axis=0), rolled)
    rolled = pltpu.roll(value, 1, 2)
    return jnp.where(lane == 0, jnp.concatenate([rolled[-1:], rolled[:-1]], axis=0), rolled)


def lane_gather(value, index):
    return jnp.take_along_axis(value, index, axis=1)


def next_chunk():
    lane = lane_iota()
    return jnp.where(lane < 64, lane + 64, jnp.where(lane == 127, 0, lane - 63))


def previous_chunk():
    lane = lane_iota()
    return jnp.where(lane >= 64, lane - 64, jnp.where(lane == 0, 127, lane + 63))


def swap_tiles_and_lanes(tiles):
    lane = lane_iota()
    for bit in range(4):
        width = 4 << bit
        high = (lane // width) % 2 == 1
        out = list(tiles)
        for m in range(16):
            if not m >> bit & 1:
                a, b = tiles[m], tiles[m | 1 << bit]
                out[m] = jnp.where(high, pltpu.roll(b, width, 1), a)
                out[m | 1 << bit] = jnp.where(high, b, pltpu.roll(a, LANES - width, 1))
        tiles = out
    return tiles


def to_chunks(tiles):
    lane = lane_iota()
    index = ((lane % 4) * 2 + lane // 64) * 16 + (lane % 64) // 4
    return swap_tiles_and_lanes([lane_gather(t, index) for t in tiles])


def from_chunks(tiles):
    lane = lane_iota()
    block = lane // 16
    index = (block % 2) * 64 + (lane % 16) * 4 + block // 2
    return [lane_gather(t, index) for t in swap_tiles_and_lanes(tiles)]


def coarse_step(count, w_in, w_out, win, values, extra, taps, sums, parts):
    lanes = win.shape[0]
    off = REACH - 4 * count
    at = [pl.ds(off + q, 8, stride=count) for q in range(count)]

    def tiles(q):
        return slice(lanes * q, lanes * q + lanes)

    for q in range(count):
        x = win[:, at[q], :]
        for dx, v in enumerate((lane_shifted(x, False), x, lane_shifted(x, True))):
            for dy in range(3):
                place = q + 1 - dy
                if place < 0:
                    taps[dy * 3 + dx, tiles(count - 1)] = pltpu.roll(v, 7, 1)
                elif place >= count:
                    taps[dy * 3 + dx, tiles(0)] = pltpu.roll(v, 1, 1)
                else:
                    taps[dy * 3 + dx, tiles(place)] = v
    total = lanes * count
    group = GROUP

    def few(i, _):
        some = pl.ds(jnp.minimum(i * group, total - group), group)
        x = taps[:, some]
        acc = None
        for h in range(8):
            hidden = jnp.tanh(jnp.sum(w_in[h][:, None] * x, axis=0))
            term = w_out[h][:, None] * hidden[None]
            acc = term if acc is None else acc + term
        sums[:, some] = acc
        return 0

    lax.fori_loop(0, -(-total // group), few, 0)
    for q in range(count):
        for dy in range(3):
            low = lane_shifted(sums[dy * 3, tiles(q)], False)
            high = lane_shifted(sums[dy * 3 + 2, tiles(q)], True)
            v = low + high + sums[dy * 3 + 1, tiles(q)]
            parts[dy, q + 1] = v
            if q == 0 and dy == 2:
                parts[dy, count + 1] = pltpu.roll(v, 7, 1)
            if q == count - 1 and dy == 0:
                parts[dy, 0] = pltpu.roll(v, 1, 1)
    for q in range(count):
        g = win[:, at[q], :] + (parts[0, q] + parts[1, q + 1] + parts[2, q + 2])
        values[:, at[q], :] = g
        if extra is not None:
            win[:, at[q], :] = g + extra(off + q, count)


def own_columns(value):
    rolled = pltpu.roll(value, 64, 2)
    lane = lax.broadcasted_iota(jnp.int32, (2, 8, LANES), 2)
    return jnp.where(lane < 64, rolled[:2], rolled[1:])


def fine_stage(src, dst, base, pcoef, qcoef, force, off, count, scale, of_base):
    at = [pl.ds(off + q, 8, stride=count) for q in range(-1, count + 1)]

    def block(first, size):
        centre = pl.ds(first, size)
        wide = [src[pl.ds(first - 1, size + 2), a, :] for a in at[1:-1]]
        column = [src[centre, at[0], :]] + [x[1:-1] for x in wide] + [src[centre, at[-1], :]]
        results = []
        for q in range(count):
            slot = (centre, at[q + 1], slice(None))
            left, right = wide[q][:-2], wide[q][2:]
            above, below = column[q + 2], column[q]
            t = pcoef[slot] * (right - left) + qcoef[slot] * (above - below) + (left + below)
            if scale != 1.0:
                t = scale * t
            here = column[q + 1] if src is base else base[slot]
            t = t + (of_base * here + force[slot])
            dst[slot] = t
            results.append(t)
        return results

    group = 10
    last = block(CHUNK - 1, 2)
    first = block(1, 2)
    block(3, group)
    ahead, back = next_chunk(), previous_chunk()
    for q in range(count):
        dst[0, at[q + 1], :] = lane_gather(last[q][1], back)
        dst[CHUNK + 1, at[q + 1], :] = lane_gather(first[q][0], ahead)

    def body(g, _):
        block(3 + g * group, group)
        return 0

    lax.fori_loop(1, (CHUNK - 4) // group, body, 0)


def fine_run(state, one, two, pcoef, qcoef, force):
    of_w, _ = fine_weights()
    for step in range(STEPS):
        count = 9 if step == 0 else 8 - step
        off = 4 if step == 0 else PAD + 4 * step
        shared = (state, pcoef, qcoef)
        fine_stage(state, one, *shared, force.at[3], off, count, 1.0, of_w[3] / of_w[4])
        fine_stage(one, two, *shared, force.at[2], off, count, 1.0, of_w[2] / of_w[4])
        fine_stage(two, one, *shared, force.at[1], off, count, 1.0, of_w[1] / of_w[4])
        fine_stage(one, state, *shared, force.at[0], PAD + 4 * step + 4, 7 - step, of_w[4], of_w[0])


def ghosts(ref):
    ahead, back = next_chunk(), previous_chunk()
    for r in range(PAD, TALL - PAD, 8):
        ref[0, r : r + 8, :] = lane_gather(ref[CHUNK, r : r + 8, :], back)
        ref[CHUNK + 1, r : r + 8, :] = lane_gather(ref[1, r : r + 8, :], ahead)


def coefficients(stream, forcing, pcoef, qcoef, force):
    of_w, of_f = fine_weights()
    ghosts(stream)
    count = 9
    at = [pl.ds(4 + q, 8, stride=count) for q in range(-1, count + 1)]

    group = 4

    def body(g, _):
        first = 1 + g * group
        c = pl.ds(first, group)
        wide = [stream[pl.ds(first - 1, group + 2), a, :] for a in at[1:-1]]
        x = [stream[c, at[0], :]] + [v[1:-1] for v in wide] + [stream[c, at[-1], :]]
        for q in range(count):
            a = at[q + 1]
            pcoef[c, a, :] = 0.5 - 1.25 * (x[q + 2] - x[q])
            qcoef[c, a, :] = 0.5 + 1.25 * (wide[q][2:] - wide[q][:-2])
            f = forcing[c, a, :]
            force[0, c, a, :] = of_f[0] * f
            for k in range(1, 4):
                force[k, c, a, :] = (of_f[k] / of_w[4]) * f
        return 0

    lax.fori_loop(0, CHUNK // group, body, 0)


def natural_to_rows(source, nat):
    for c in range(64):
        nat[c * PITCH : c * PITCH + INNER, :] = source[:, c * LANES : (c + 1) * LANES]


def rows_to_chunks(nat, lam):
    low = lax.broadcasted_iota(jnp.int32, (64, LANES), 1) < 64
    for i in range(INNER // 2):
        j = i + INNER // 2
        at_i, at_j = pl.ds(i, 64, stride=PITCH), pl.ds(j, 64, stride=PITCH)
        flipped = jnp.concatenate([nat[at_i, :], nat[at_j, :]], axis=0).T
        top, bottom = flipped[:64], flipped[64:]
        lam[at_i, :] = jnp.where(low, top, pltpu.roll(bottom, 64, 1))
        lam[at_j, :] = jnp.where(low, pltpu.roll(top, 64, 1), bottom)


def chunks_to_rows(lam, nat):
    low = lax.broadcasted_iota(jnp.int32, (64, LANES), 1) < 64
    for i in range(INNER // 2):
        j = i + INNER // 2
        at_i, at_j = pl.ds(i, 64, stride=PITCH), pl.ds(j, 64, stride=PITCH)
        x, y = lam[at_i, :], lam[at_j, :]
        top = jnp.where(low, x, pltpu.roll(y, 64, 1))
        bottom = jnp.where(low, pltpu.roll(x, 64, 1), y)
        flipped = jnp.concatenate([top, bottom], axis=0).T
        nat[at_i, :] = flipped[:64]
        nat[at_j, :] = flipped[64:]


def store_own(lam, ref):
    for c in range(CHUNK):
        ref[1 + c, OWN : OWN + INNER, :] = lam[c * PITCH : c * PITCH + INNER, :]


def load_own(ref, lam):
    for c in range(CHUNK):
        lam[c * PITCH : c * PITCH + INNER, :] = ref[1 + c, OWN : OWN + INNER, :]


def spaced_tiles(tiles, rolled):
    lane = lane_iota()
    turned = [pltpu.roll(t, 64, 1) for t in tiles]
    for k in range(BLOCKS):
        v = jnp.where(lane < 64, turned[k - 1], turned[k])
        rolled[k] = v
        if k < 2:
            rolled[BLOCKS + k] = v


def block_means(state):
    tiles = []
    for m in range(BLOCKS):
        four = [state[1 + 4 * m : 5 + 4 * m, pl.ds(OWN + q, 8, stride=4), :] for q in range(4)]
        tiles.append(0.0625 * jnp.sum((four[0] + four[1]) + (four[2] + four[3]), axis=0))
    return from_chunks(tiles)


def coarse_in_chunks(pieces, coarse):
    for half in range(2):
        at = pl.ds(half, 8, stride=2)
        tiles = to_chunks([pieces[m // 2, m % 2, at, :] for m in range(BLOCKS)])
        for m in range(BLOCKS):
            coarse[m, at, :] = tiles[m]


def spread_coarse(coarse, base, state):
    upper = lax.broadcasted_iota(jnp.int32, (8, LANES), 0) < 4

    def body(m, _):
        c = pl.ds(4 * m, 4)
        for r in range(8):
            v = jnp.where(upper, coarse[m, 2 * r : 2 * r + 1, :], coarse[m, 2 * r + 1 : 2 * r + 2, :])[None]
            old = base(c, r)
            v = jnp.broadcast_to(v, (4, 8, LANES)) if old is None else old + v
            state[pl.ds(4 * m + 1, 4), PAD + 8 * r : PAD + 8 * r + 8, :] = v
        return 0

    lax.fori_loop(0, BLOCKS, body, 0)


GROUP = 3
AHEAD = 24
FIRST_PART, SECOND_PART = 1, 4


def kernel(
    conv_in, conv_out, vort_hbm, stream_hbm, force_hbm, out, delta_out,
    inputs, nat, lam, fields, state, one, two, pcoef, qcoef, force,
    start, win, old, new, taps, sums, parts, w_in, w_out,
    rolled, means, sent, got, edge, coarse, packed,
    in_sem, send_sem, recv_sem,
):
    t, z = lax.axis_index("tm"), lax.axis_index("space")
    slabs = lax.axis_size("space")
    parity = lax.rem(t, 2)
    used = [0]

    def slot_of(k):
        return lax.rem(t + k, SLICES)

    def slab_of(d):
        return lax.rem(z + d + slabs, slabs)

    def reserve(count):
        used[0] += count
        return used[0] - count

    def remote(src, dst, to, send=None, recv=None):
        if send is None:
            send = recv = reserve(1)
        return pltpu.make_async_remote_copy(
            src_ref=src, dst_ref=dst, send_sem=send_sem.at[send], recv_sem=recv_sem.at[recv],
            device_id=to, device_id_type=MESH,
        )

    def start_all(copies):
        for c in copies:
            c.start()

    def recv_all(copies):
        for c in copies:
            c.wait_recv()

    def sent_all(copies):
        for c in copies:
            c.wait_send()

    loads = [
        pltpu.make_async_copy(ref, inputs.at[i], in_sem.at[i])
        for i, ref in enumerate((vort_hbm, stream_hbm, force_hbm))
    ]
    start_all(loads)
    barrier = pltpu.get_barrier_semaphore()
    peers = [(slot_of(k), z) for k in range(1, SLICES)] + [(t, slab_of(d)) for d in (-3, -2, -1, 1, 2, 3)]
    for p in peers:
        pl.semaphore_signal(barrier, inc=1, device_id=p, device_id_type=MESH)
    for dy in range(3):
        v_in, v_out = conv_in[dy], 0.5 * conv_out[dy]
        for dx in range(3):
            for h in range(8):
                w_in[h, dy * 3 + dx] = jnp.broadcast_to(v_in[dx : dx + 1, h : h + 1], (8, LANES))
                w_out[h, dy * 3 + dx] = jnp.broadcast_to(v_out[dx : dx + 1, h : h + 1], (8, LANES))

    loads[0].wait()
    natural_to_rows(inputs.at[0], nat)
    for c in range(64):
        four = [nat[pl.ds(c * PITCH + q, 8, stride=4), :] for q in range(4)]
        m, k = c // 4, c % 4
        packed[m * 8 : m * 8 + 8, k * LANES : (k + 1) * LANES] = (four[0] + four[1]) + (four[2] + four[3])
    averages = jnp.where(
        lax.broadcasted_iota(jnp.int32, (4 * LANES, LANES), 0) // 4
        == lax.broadcasted_iota(jnp.int32, (4 * LANES, LANES), 1), 0.0625, 0.0,
    ).astype(F32)
    first = jnp.dot(packed[...], averages, precision=HIGH, preferred_element_type=F32)
    spaced_tiles([first[m * 8 : m * 8 + 8] for m in range(BLOCKS)], rolled.at[0])
    mine = pl.ds(2 * t, 3)
    near = [
        remote(rolled.at[0, mine], start.at[:, REACH - 4 - 8 * d : REACH + 4 - 8 * d, :], (t, slab_of(d)))
        for d in (-1, 1, -2, 2, -3, 3)
    ]

    @pl.when(t == 1)
    def _():
        rows_to_chunks(nat, lam)
        store_own(lam, state)

    inside = slice(1, CHUNK + 1)
    low, high = slice(OWN - HALO, OWN), slice(OWN + INNER, OWN + INNER + HALO)
    first_rows, last_rows = slice(OWN, OWN + HALO), slice(OWN + INNER - HALO, OWN + INNER)
    sibling = (t + 1 - 2 * parity, z)
    half = lax.rem(t // 2, 2)
    size = CHUNK // 4

    def part_of(which, part):
        return pl.ds(1 + 2 * size * which + size * part, size)

    across, helped, shared = [], [], [[], []]
    for part in range(2):
        some = part_of(half, part)
        across.append(
            [
                remote(fields.at[parity, some, last_rows], fields.at[parity, some, low], (t, slab_of(1))),
                remote(fields.at[parity, some, first_rows], fields.at[parity, some, high], (t, slab_of(-1))),
            ]
        )
        helped.append(
            [
                remote(fields.at[parity, some, rows], fields.at[parity, some, rows], (slot_of(k), z))
                for rows, k in ((low, SLICES - 2), (high, 2))
            ]
        )
        for k, which in enumerate((half, 1 - half)):
            some = part_of(which, part)
            shared[k].append(
                [remote(fields.at[parity, some, rows], fields.at[parity, some, rows], sibling) for rows in (low, high)]
            )
    early = [
        remote(state.at[inside, last_rows], state.at[inside, low], (t, slab_of(1))),
        remote(state.at[inside, first_rows], state.at[inside, high], (t, slab_of(-1))),
    ]
    loads[1].wait()
    loads[2].wait()

    def lay_out(which):
        natural_to_rows(inputs.at[1 + which], nat)
        rows_to_chunks(nat, lam)
        store_own(lam, fields.at[which])

    lay_out(parity)
    pl.semaphore_wait(barrier, len(peers))
    start_all(near)

    start_all(across[0])
    start_all(across[1])

    @pl.when(t == 1)
    def _():
        start_all(early)

    start[:, REACH - 4 : REACH + 4, :] = rolled[0, mine]
    lay_out(1 - parity)

    recv_all(near)
    win[...] = start[...]
    scratch = (taps, sums, parts)

    def rows_of(ref):
        return lambda r: ref[:, r : r + 8, :]

    def change(a, b):
        return lambda r: a[:, r : r + 8, :] - b[:, r : r + 8, :]

    def deliverer(phase, rows):
        send, recv = reserve(SLICES), reserve(SLICES)
        here = slice(0, rows)

        def copy(n, to, source):
            return remote(
                sent.at[phase, n, :, here], got.at[phase, source, :, here], (to, z), send + n, recv + source
            )

        def put(n, to, read):
            for r in range(0, rows, 8):
                sent[phase, n, :, r : r + 8, :] = own_columns(read(REACH - rows // 2 + r))

            @pl.when(t != to)
            def _():
                copy(n, to, t).start()

            @pl.when(t == to)
            def _():
                got[phase, t, :, here, :] = sent[phase, n, :, here, :]

        def take():
            @pl.when(t > 1)
            def _():
                for k in range(1, SLICES):
                    copy(2, 2, slot_of(k)).wait_recv()

        def done(pairs):
            for n, to in pairs:
                @pl.when(t != to)
                def _():
                    copy(n, to, t).wait_send()

        return put, take, done

    plain = lambda row, count: 0.0
    put_0, take_0, done_0 = deliverer(0, 16)
    for n in range(8):
        coarse_step(-(-(44 - 4 * n) // 8), w_in, w_out, win, old.at[n], plain if n < 7 else None, *scratch)
        if n < 6:
            put_0(n + 1, n + 2, rows_of(win))
        if n == FIRST_PART or n == SECOND_PART:
            part = int(n == SECOND_PART)
            recv_all(across[part])
            start_all(helped[part])
            start_all(shared[0][part])
        if n >= 6:
            recv_all(helped[n - 6])
            start_all(shared[1][n - 6])

    take_0()

    @pl.when(t > 1)
    def _():
        coarse_in_chunks(got.at[0], coarse)
        spread_coarse(coarse, lambda c, r: None, state)

    for copies in shared:
        for part in range(2):
            recv_all(copies[part])
    coefficients(fields.at[0], fields.at[1], pcoef, qcoef, force)

    @pl.when(t == 1)
    def _():
        recv_all(early)
        sent_all(early)

    @pl.when(t > 0)
    def _():
        ghosts(state)
        fine_run(state, one, two, pcoef, qcoef, force)

    def sharer(phase, shift, wanted, wanted_two):
        place = lax.rem(t + shift, SLICES)
        middle = slice(16, 24)
        send, recv, around = reserve(SLICES), reserve(SLICES), reserve(4 * SLICES)

        def copy(k, slot):
            return remote(
                rolled.at[phase + 1, pl.ds(2 * slot_of(k), 3)], means.at[phase, slot, :, middle],
                (slot_of(k), z), send + k, recv + slot,
            )

        def spread(n):
            return [
                remote(
                    means.at[phase, n, :, middle], means.at[phase, n, :, 16 - 8 * d : 24 - 8 * d],
                    (t, slab_of(d)), around + 4 * n + j, around + 4 * n + j,
                )
                for j, d in enumerate((-1, 1, -2, 2))
                if abs(d) == 1 or n in wanted_two
            ]

        has_slice = functools.reduce(jnp.logical_or, [place == n for n in wanted])

        def go():
            @pl.when(has_slice)
            def _():
                spaced_tiles(block_means(state), rolled.at[phase + 1])
                for k in range(1, SLICES):
                    copy(k, place).start()
                means[phase, place, :, middle, :] = rolled[phase + 1, pl.ds(2 * t, 3)]

        def pass_on():
            for n in wanted:
                @pl.when(place != n)
                def _():
                    copy(1, n).wait_recv()

                start_all(spread(n))

        def take(n):
            recv_all(spread(n))

        def done():
            @pl.when(has_slice)
            def _():
                for k in range(1, SLICES):
                    copy(k, place).wait_send()

            for n in wanted:
                sent_all(spread(n))

        return go, pass_on, take, done

    go_1, pass_1, arrived_1, shared_1 = sharer(0, SLICES - 1, range(0, 7), range(0, 4))
    go_1()
    copy_f = remote(state.at[inside, slice(OWN, OWN + INNER)], one.at[inside, slice(OWN, OWN + INNER)], (0, z))

    @pl.when(t == 1)
    def _():
        copy_f.start()

    bulk = [
        remote(state.at[1 + a : 1 + b, rows], edge.at[side, a:b], (t, slab_of(1 - 2 * side)))
        for a, b in ((0, AHEAD), (AHEAD, CHUNK))
        for side, rows in enumerate((last_rows, first_rows))
    ]

    @pl.when(t > 0)
    def _():
        start_all(bulk[:2])

    pass_1()

    @pl.when(t > 0)
    def _():
        start_all(bulk[2:])

    def corrected(phase, n, before):
        def extra(row, count):
            there = pl.ds(row - 8, 8, stride=count)
            return means[phase, n, :, there, :] - before[n, :, pl.ds(row, 8, stride=count), :]

        return extra

    put_1, take_1, done_1 = deliverer(1, 16)
    arrived_1(0)
    win[:, 8:48, :] = means[0, 0]
    for n in range(1, 8):
        if n < 7:
            arrived_1(n)
        coarse_step(
            -(-(44 - 4 * n) // 8), w_in, w_out, win, new.at[n], corrected(0, n, old) if n < 7 else None, *scratch
        )
        if n < 7:
            put_1(n, n + 1, change(new.at[n], old.at[n]))

    take_1()

    @pl.when(t == 1)
    def _():
        copy_f.wait_send()
        got[1] = jnp.zeros(got.shape[1:], F32)

    @pl.when(t > 0)
    def _():
        recv_all(bulk)
        sent_all(bulk)
        coarse_in_chunks(got.at[1], coarse)

        def base(c, r):
            if r < 2:
                return edge[0, c, 8 * r : 8 * r + 8, :]
            if r >= 6:
                return edge[1, c, 8 * (r - 6) : 8 * (r - 6) + 8, :]
            return state[pl.ds(c.start + 1, 4), PAD + 8 * r : PAD + 8 * r + 8, :]

        spread_coarse(coarse, base, state)
        ghosts(state)
        fine_run(state, one, two, pcoef, qcoef, force)

    go_2, pass_2, arrived_2, shared_2 = sharer(1, 0, range(1, 7), range(1, 3))
    go_2()
    pass_2()

    @pl.when(t == 0)
    def _():
        copy_f.wait_recv()
        load_own(one, lam)

    @pl.when(t > 0)
    def _():
        load_own(state, lam)

    put_2, take_2, done_2 = deliverer(2, 8)
    arrived_2(1)
    win[:, 8:48, :] = means[1, 1]
    for n in range(2, 8):
        if n < 7:
            arrived_2(n)
        coarse_step(
            -(-(40 - 4 * n) // 8), w_in, w_out, win, old.at[n], corrected(1, n, new) if n < 7 else None, *scratch
        )
        put_2(n, n, change(old.at[n], new.at[n]))

    chunks_to_rows(lam, nat)
    for c in range(64):
        inputs[0, :, c * LANES : (c + 1) * LANES] = nat[c * PITCH : c * PITCH + INNER, :]
    store = pltpu.make_async_copy(inputs.at[0], out, in_sem.at[0])
    store.start()

    @pl.when(t <= 1)
    def _():
        got[2] = jnp.zeros(got.shape[1:], F32)

    sent_all(near)
    for part in range(2):
        sent_all(across[part])
        sent_all(helped[part])
        sent_all(shared[0][part])
        sent_all(shared[1][part])
    done_0([(n, n + 1) for n in range(1, 7)])
    done_1([(n, n + 1) for n in range(1, 7)])
    done_2([(n, n) for n in range(2, 8)])
    shared_1()
    shared_2()
    take_2()
    for m in range(BLOCKS):
        delta_out[m * 8 : m * 8 + 8, :] = got[2, m // 2, m % 2, 0:8, :]
    store.wait()


def finish_kernel(fine, delta, out):
    copies = jnp.where(
        lax.broadcasted_iota(jnp.int32, (LANES, 4 * LANES), 0)
        == lax.broadcasted_iota(jnp.int32, (LANES, 4 * LANES), 1) // 4, 1.0, 0.0,
    ).astype(F32)
    wide = jnp.dot(delta[...], copies, precision=HIGH, preferred_element_type=F32)
    upper = lax.broadcasted_iota(jnp.int32, (8, 4 * LANES), 0) < 4
    for m in range(delta.shape[0] // 8):
        cols = slice(m * 4 * LANES, (m + 1) * 4 * LANES)
        for a in range(INNER // 8):
            r = m * 8 + 2 * a
            v = jnp.where(upper, wide[r : r + 1], wide[r + 1 : r + 2])
            out[0, a * 8 : a * 8 + 8, cols] = fine[a * 8 : a * 8 + 8, cols] + v


def body(vorticity, stream, forcing, conv_in, conv_out):
    rows, cols = vorticity.shape
    whole = (CHUNK + 2, TALL, LANES)
    vmem = pl.BlockSpec(memory_space=VMEM)
    anywhere = pl.BlockSpec(memory_space=pl.ANY)
    window = (3, WINDOW, LANES)
    shapes = [
        (3, rows, cols), (64 * PITCH, LANES), (CHUNK * PITCH, LANES), (2,) + whole, whole, whole, whole, whole, whole,
        (4,) + whole, window, window, (SLICES,) + window, (SLICES,) + window,
        (9, 18, 8, LANES), (9, 18, 8, LANES), (3, 8, 3, 8, LANES), (8, 9, 8, LANES), (8, 9, 8, LANES),
        (3, BLOCKS + 2, 8, LANES), (2, SLICES, 3, 40, LANES), (3, SLICES, 2, 16, LANES), (3, SLICES, 2, 16, LANES),
        (2, CHUNK, HALO, LANES), (BLOCKS, 16, LANES), (8 * BLOCKS, 4 * LANES),
    ]
    slots = 176
    fine, delta = pl.pallas_call(
        kernel,
        name="parareal",
        out_shape=(jax.ShapeDtypeStruct((rows, cols), F32), jax.ShapeDtypeStruct((8 * BLOCKS, LANES), F32)),
        in_specs=[vmem, vmem, anywhere, anywhere, anywhere],
        out_specs=(anywhere, vmem),
        scratch_shapes=[VMEM(s, F32) for s in shapes]
        + [pltpu.SemaphoreType.DMA((3,)), pltpu.SemaphoreType.DMA((slots,)), pltpu.SemaphoreType.DMA((slots,))],
        compiler_params=pltpu.CompilerParams(vmem_limit_bytes=62 * 2**20, collective_id=0, has_side_effects=True),
    )(jnp.transpose(conv_in, (1, 2, 0)), jnp.transpose(conv_out, (1, 2, 0)), vorticity, stream, forcing)
    grid = 2
    return pl.pallas_call(
        finish_kernel,
        name="finish",
        grid=(grid,),
        out_shape=jax.ShapeDtypeStruct((1, rows, cols), F32),
        in_specs=[
            pl.BlockSpec((rows, cols // grid), lambda i: (0, i)),
            pl.BlockSpec((8 * BLOCKS // grid, LANES), lambda i: (i, 0)),
        ],
        out_specs=pl.BlockSpec((1, rows, cols // grid), lambda i: (0, 0, i)),
    )(fine, delta)


def solution(mesh):
    placed = (P("space", None), P("space", None), P("space", None), P(), P())
    return jax.shard_map(
        body, mesh=mesh, in_specs=placed, out_specs=P("tm", "space", None), check_vma=False
    )
```

```python
import functools
import math

import jax
import jax.numpy as jnp
import numpy as np
from jax import lax
from jax.experimental import pallas as pl
from jax.experimental.pallas import tpu as pltpu
from jax.sharding import PartitionSpec as P

F32 = jnp.float32
VMEM = pltpu.VMEM
MESH = pl.DeviceIdType.MESH
HIGH = lax.Precision.HIGHEST

STEPS = 4
SLICES = 8
LANES = 128
CHUNK = 64
INNER = 32
HALO = 16
PAD = 8
TALL = INNER + 2 * HALO + 2 * PAD
OWN = PAD + HALO
PITCH = 33
BLOCKS = 16
REACH = 28
WINDOW = 2 * REACH


def fine_weights():
    shift = np.polynomial.Polynomial([-0.45, 0.2])
    of_w = sum(shift**j / math.factorial(j) for j in range(5))
    of_f = sum(shift**j / math.factorial(j + 1) for j in range(4))
    return [float(v) for v in of_w.coef], [float(v) for v in of_f.coef] + [0.0]


def lane_iota():
    return lax.broadcasted_iota(jnp.int32, (8, LANES), 1)


def lane_shifted(value, up):
    lane = lax.broadcasted_iota(jnp.int32, value.shape, 2)
    if up:
        rolled = pltpu.roll(value, LANES - 1, 2)
        return jnp.where(lane == LANES - 1, jnp.concatenate([rolled[1:], rolled[:1]], axis=0), rolled)
    rolled = pltpu.roll(value, 1, 2)
    return jnp.where(lane == 0, jnp.concatenate([rolled[-1:], rolled[:-1]], axis=0), rolled)


def lane_gather(value, index):
    return jnp.take_along_axis(value, index, axis=1)


def next_chunk():
    lane = lane_iota()
    return jnp.where(lane < 64, lane + 64, jnp.where(lane == 127, 0, lane - 63))


def previous_chunk():
    lane = lane_iota()
    return jnp.where(lane >= 64, lane - 64, jnp.where(lane == 0, 127, lane + 63))


def swap_tiles_and_lanes(tiles):
    lane = lane_iota()
    for bit in range(4):
        width = 4 << bit
        high = (lane // width) % 2 == 1
        out = list(tiles)
        for m in range(16):
            if not m >> bit & 1:
                a, b = tiles[m], tiles[m | 1 << bit]
                out[m] = jnp.where(high, pltpu.roll(b, width, 1), a)
                out[m | 1 << bit] = jnp.where(high, b, pltpu.roll(a, LANES - width, 1))
        tiles = out
    return tiles


def to_chunks(tiles):
    lane = lane_iota()
    index = ((lane % 4) * 2 + lane // 64) * 16 + (lane % 64) // 4
    return swap_tiles_and_lanes([lane_gather(t, index) for t in tiles])


def from_chunks(tiles):
    lane = lane_iota()
    block = lane // 16
    index = (block % 2) * 64 + (lane % 16) * 4 + block // 2
    return [lane_gather(t, index) for t in swap_tiles_and_lanes(tiles)]


def coarse_step(count, w_in, w_out, win, values, extra, taps, sums, parts):
    lanes = win.shape[0]
    off = REACH - 4 * count
    at = [pl.ds(off + q, 8, stride=count) for q in range(count)]

    def tiles(q):
        return slice(lanes * q, lanes * q + lanes)

    for q in range(count):
        x = win[:, at[q], :]
        for dx, v in enumerate((lane_shifted(x, False), x, lane_shifted(x, True))):
            for dy in range(3):
                place = q + 1 - dy
                if place < 0:
                    taps[dy * 3 + dx, tiles(count - 1)] = pltpu.roll(v, 7, 1)
                elif place >= count:
                    taps[dy * 3 + dx, tiles(0)] = pltpu.roll(v, 1, 1)
                else:
                    taps[dy * 3 + dx, tiles(place)] = v
    total = lanes * count
    group = GROUP

    def few(i, _):
        some = pl.ds(jnp.minimum(i * group, total - group), group)
        x = taps[:, some]
        acc = None
        for h in range(8):
            hidden = jnp.tanh(jnp.sum(w_in[h][:, None] * x, axis=0))
            term = w_out[h][:, None] * hidden[None]
            acc = term if acc is None else acc + term
        sums[:, some] = acc
        return 0

    lax.fori_loop(0, -(-total // group), few, 0)
    for q in range(count):
        for dy in range(3):
            low = lane_shifted(sums[dy * 3, tiles(q)], False)
            high = lane_shifted(sums[dy * 3 + 2, tiles(q)], True)
            v = low + high + sums[dy * 3 + 1, tiles(q)]
            parts[dy, q + 1] = v
            if q == 0 and dy == 2:
                parts[dy, count + 1] = pltpu.roll(v, 7, 1)
            if q == count - 1 and dy == 0:
                parts[dy, 0] = pltpu.roll(v, 1, 1)
    for q in range(count):
        g = win[:, at[q], :] + (parts[0, q] + parts[1, q + 1] + parts[2, q + 2])
        values[:, at[q], :] = g
        if extra is not None:
            win[:, at[q], :] = g + extra(off + q, count)


def own_columns(value):
    rolled = pltpu.roll(value, 64, 2)
    lane = lax.broadcasted_iota(jnp.int32, (2, 8, LANES), 2)
    return jnp.where(lane < 64, rolled[:2], rolled[1:])


def fine_stage(src, dst, base, pcoef, qcoef, force, off, count, scale, of_base):
    at = [pl.ds(off + q, 8, stride=count) for q in range(-1, count + 1)]

    def block(first, size):
        centre = pl.ds(first, size)
        wide = [src[pl.ds(first - 1, size + 2), a, :] for a in at[1:-1]]
        column = [src[centre, at[0], :]] + [x[1:-1] for x in wide] + [src[centre, at[-1], :]]
        results = []
        for q in range(count):
            slot = (centre, at[q + 1], slice(None))
            left, right = wide[q][:-2], wide[q][2:]
            above, below = column[q + 2], column[q]
            t = pcoef[slot] * (right - left) + qcoef[slot] * (above - below) + (left + below)
            if scale != 1.0:
                t = scale * t
            here = column[q + 1] if src is base else base[slot]
            t = t + (of_base * here + force[slot])
            dst[slot] = t
            results.append(t)
        return results

    group = 10
    last = block(CHUNK - 1, 2)
    first = block(1, 2)
    block(3, group)
    ahead, back = next_chunk(), previous_chunk()
    for q in range(count):
        dst[0, at[q + 1], :] = lane_gather(last[q][1], back)
        dst[CHUNK + 1, at[q + 1], :] = lane_gather(first[q][0], ahead)

    def body(g, _):
        block(3 + g * group, group)
        return 0

    lax.fori_loop(1, (CHUNK - 4) // group, body, 0)


def fine_run(state, one, two, pcoef, qcoef, force):
    of_w, _ = fine_weights()
    for step in range(STEPS):
        count = 9 if step == 0 else 8 - step
        off = 4 if step == 0 else PAD + 4 * step
        shared = (state, pcoef, qcoef)
        fine_stage(state, one, *shared, force.at[3], off, count, 1.0, of_w[3] / of_w[4])
        fine_stage(one, two, *shared, force.at[2], off, count, 1.0, of_w[2] / of_w[4])
        fine_stage(two, one, *shared, force.at[1], off, count, 1.0, of_w[1] / of_w[4])
        fine_stage(one, state, *shared, force.at[0], PAD + 4 * step + 4, 7 - step, of_w[4], of_w[0])


def ghosts(ref, rows=range(PAD, TALL - PAD, 8)):
    ahead, back = next_chunk(), previous_chunk()
    for r in rows:
        ref[0, r : r + 8, :] = lane_gather(ref[CHUNK, r : r + 8, :], back)
        ref[CHUNK + 1, r : r + 8, :] = lane_gather(ref[1, r : r + 8, :], ahead)


def coefficients(stream, forcing, pcoef, qcoef, force, of_stream, of_forcing):
    of_w, of_f = fine_weights()
    ghosts(stream, of_stream)
    group = 4

    def body(g, _):
        first = 1 + g * group
        c = pl.ds(first, group)
        for r in of_stream:
            rows = slice(r, r + 8)
            wide = stream[pl.ds(first - 1, group + 2), rows, :]
            pcoef[c, rows, :] = 0.5 - 1.25 * (stream[c, r + 1 : r + 9, :] - stream[c, r - 1 : r + 7, :])
            qcoef[c, rows, :] = 0.5 + 1.25 * (wide[2:] - wide[:-2])
        for r in of_forcing:
            rows = slice(r, r + 8)
            f = forcing[c, rows, :]
            force[0, c, rows, :] = of_f[0] * f
            for k in range(1, 4):
                force[k, c, rows, :] = (of_f[k] / of_w[4]) * f
        return 0

    lax.fori_loop(0, CHUNK // group, body, 0)


def natural_to_rows(source, nat):
    for c in range(64):
        nat[c * PITCH : c * PITCH + INNER, :] = source[:, c * LANES : (c + 1) * LANES]


def rows_to_chunks(nat, lam):
    low = lax.broadcasted_iota(jnp.int32, (64, LANES), 1) < 64
    for i in range(INNER // 2):
        j = i + INNER // 2
        at_i, at_j = pl.ds(i, 64, stride=PITCH), pl.ds(j, 64, stride=PITCH)
        flipped = jnp.concatenate([nat[at_i, :], nat[at_j, :]], axis=0).T
        top, bottom = flipped[:64], flipped[64:]
        lam[at_i, :] = jnp.where(low, top, pltpu.roll(bottom, 64, 1))
        lam[at_j, :] = jnp.where(low, pltpu.roll(top, 64, 1), bottom)


def chunks_to_rows(lam, nat):
    low = lax.broadcasted_iota(jnp.int32, (64, LANES), 1) < 64
    for i in range(INNER // 2):
        j = i + INNER // 2
        at_i, at_j = pl.ds(i, 64, stride=PITCH), pl.ds(j, 64, stride=PITCH)
        x, y = lam[at_i, :], lam[at_j, :]
        top = jnp.where(low, x, pltpu.roll(y, 64, 1))
        bottom = jnp.where(low, pltpu.roll(x, 64, 1), y)
        flipped = jnp.concatenate([top, bottom], axis=0).T
        nat[at_i, :] = flipped[:64]
        nat[at_j, :] = flipped[64:]


def store_own(lam, ref):
    for c in range(CHUNK):
        ref[1 + c, OWN : OWN + INNER, :] = lam[c * PITCH : c * PITCH + INNER, :]


def load_own(ref, lam):
    for c in range(CHUNK):
        lam[c * PITCH : c * PITCH + INNER, :] = ref[1 + c, OWN : OWN + INNER, :]


def spaced_tiles(tiles, rolled):
    lane = lane_iota()
    turned = [pltpu.roll(t, 64, 1) for t in tiles]
    for k in range(BLOCKS):
        v = jnp.where(lane < 64, turned[k - 1], turned[k])
        rolled[k] = v
        if k < 2:
            rolled[BLOCKS + k] = v


def block_means(state):
    tiles = []
    for m in range(BLOCKS):
        four = [state[1 + 4 * m : 5 + 4 * m, pl.ds(OWN + q, 8, stride=4), :] for q in range(4)]
        tiles.append(0.0625 * jnp.sum((four[0] + four[1]) + (four[2] + four[3]), axis=0))
    return from_chunks(tiles)


def coarse_in_chunks(pieces, coarse):
    for half in range(2):
        at = pl.ds(half, 8, stride=2)
        tiles = to_chunks([pieces[m // 2, m % 2, at, :] for m in range(BLOCKS)])
        for m in range(BLOCKS):
            coarse[m, at, :] = tiles[m]


def spread_coarse(coarse, base, state):
    upper = lax.broadcasted_iota(jnp.int32, (8, LANES), 0) < 4

    def body(m, _):
        c = pl.ds(4 * m, 4)
        for r in range(8):
            v = jnp.where(upper, coarse[m, 2 * r : 2 * r + 1, :], coarse[m, 2 * r + 1 : 2 * r + 2, :])[None]
            old = base(c, r)
            v = jnp.broadcast_to(v, (4, 8, LANES)) if old is None else old + v
            state[pl.ds(4 * m + 1, 4), PAD + 8 * r : PAD + 8 * r + 8, :] = v
        return 0

    lax.fori_loop(0, BLOCKS, body, 0)


GROUP = 3
AHEAD = 24
FIRST_PART, SECOND_PART = 1, 4


def kernel(
    conv_in, conv_out, vort_hbm, stream_hbm, force_hbm, out, delta_out,
    inputs, nat, lam, fields, state, one, two, pcoef, qcoef, force,
    start, win, old, new, taps, sums, parts, w_in, w_out,
    rolled, means, sent, got, edge, coarse, packed,
    in_sem, send_sem, recv_sem,
):
    t, z = lax.axis_index("tm"), lax.axis_index("space")
    slabs = lax.axis_size("space")
    parity = lax.rem(t, 2)
    used = [0]

    def slot_of(k):
        return lax.rem(t + k, SLICES)

    def slab_of(d):
        return lax.rem(z + d + slabs, slabs)

    def reserve(count):
        used[0] += count
        return used[0] - count

    def remote(src, dst, to, send=None, recv=None):
        if send is None:
            send = recv = reserve(1)
        return pltpu.make_async_remote_copy(
            src_ref=src, dst_ref=dst, send_sem=send_sem.at[send], recv_sem=recv_sem.at[recv],
            device_id=to, device_id_type=MESH,
        )

    def start_all(copies):
        for c in copies:
            c.start()

    def recv_all(copies):
        for c in copies:
            c.wait_recv()

    def sent_all(copies):
        for c in copies:
            c.wait_send()

    loads = [
        pltpu.make_async_copy(ref, inputs.at[i], in_sem.at[i])
        for i, ref in enumerate((vort_hbm, stream_hbm, force_hbm))
    ]
    start_all(loads)
    barrier = pltpu.get_barrier_semaphore()
    peers = [(slot_of(k), z) for k in range(1, SLICES)] + [(t, slab_of(d)) for d in (-3, -2, -1, 1, 2, 3)]
    for p in peers:
        pl.semaphore_signal(barrier, inc=1, device_id=p, device_id_type=MESH)
    for dy in range(3):
        v_in, v_out = conv_in[dy], 0.5 * conv_out[dy]
        for dx in range(3):
            for h in range(8):
                w_in[h, dy * 3 + dx] = jnp.broadcast_to(v_in[dx : dx + 1, h : h + 1], (8, LANES))
                w_out[h, dy * 3 + dx] = jnp.broadcast_to(v_out[dx : dx + 1, h : h + 1], (8, LANES))

    loads[0].wait()
    natural_to_rows(inputs.at[0], nat)
    for c in range(64):
        four = [nat[pl.ds(c * PITCH + q, 8, stride=4), :] for q in range(4)]
        m, k = c // 4, c % 4
        packed[m * 8 : m * 8 + 8, k * LANES : (k + 1) * LANES] = (four[0] + four[1]) + (four[2] + four[3])
    averages = jnp.where(
        lax.broadcasted_iota(jnp.int32, (4 * LANES, LANES), 0) // 4
        == lax.broadcasted_iota(jnp.int32, (4 * LANES, LANES), 1), 0.0625, 0.0,
    ).astype(F32)
    first = jnp.dot(packed[...], averages, precision=HIGH, preferred_element_type=F32)
    spaced_tiles([first[m * 8 : m * 8 + 8] for m in range(BLOCKS)], rolled.at[0])
    mine = pl.ds(2 * t, 3)
    near = [
        remote(rolled.at[0, mine], start.at[:, REACH - 4 - 8 * d : REACH + 4 - 8 * d, :], (t, slab_of(d)))
        for d in (-1, 1, -2, 2, -3, 3)
    ]

    @pl.when(t == 1)
    def _():
        rows_to_chunks(nat, lam)
        store_own(lam, state)

    inside = slice(1, CHUNK + 1)
    low, high = slice(OWN - HALO, OWN), slice(OWN + INNER, OWN + INNER + HALO)
    first_rows, last_rows = slice(OWN, OWN + HALO), slice(OWN + INNER - HALO, OWN + INNER)
    sibling = (t + 1 - 2 * parity, z)
    half = lax.rem(t // 2, 2)
    size = CHUNK // 4

    def part_of(which, part):
        return pl.ds(1 + 2 * size * which + size * part, size)

    across, helped, shared = [], [], [[], []]
    for part in range(2):
        some = part_of(half, part)
        across.append(
            [
                remote(fields.at[parity, some, last_rows], fields.at[parity, some, low], (t, slab_of(1))),
                remote(fields.at[parity, some, first_rows], fields.at[parity, some, high], (t, slab_of(-1))),
            ]
        )
        helped.append(
            [
                remote(fields.at[parity, some, rows], fields.at[parity, some, rows], (slot_of(k), z))
                for rows, k in ((low, SLICES - 2), (high, 2))
            ]
        )
        for k, which in enumerate((half, 1 - half)):
            some = part_of(which, part)
            shared[k].append(
                [remote(fields.at[parity, some, rows], fields.at[parity, some, rows], sibling) for rows in (low, high)]
            )
    early = [
        remote(state.at[inside, last_rows], state.at[inside, low], (t, slab_of(1))),
        remote(state.at[inside, first_rows], state.at[inside, high], (t, slab_of(-1))),
    ]
    loads[1].wait()
    loads[2].wait()

    def lay_out(which):
        natural_to_rows(inputs.at[1 + which], nat)
        rows_to_chunks(nat, lam)
        store_own(lam, fields.at[which])

    lay_out(parity)
    pl.semaphore_wait(barrier, len(peers))
    start_all(near)

    start_all(across[0])
    start_all(across[1])

    @pl.when(t == 1)
    def _():
        start_all(early)

    start[:, REACH - 4 : REACH + 4, :] = rolled[0, mine]
    lay_out(1 - parity)
    coefficients(fields.at[0], fields.at[1], pcoef, qcoef, force, (32, 40), (24, 32, 40, 48))

    recv_all(near)
    win[...] = start[...]
    scratch = (taps, sums, parts)

    def rows_of(ref):
        return lambda r: ref[:, r : r + 8, :]

    def change(a, b):
        return lambda r: a[:, r : r + 8, :] - b[:, r : r + 8, :]

    def deliverer(phase, rows):
        send, recv = reserve(SLICES), reserve(SLICES)
        here = slice(0, rows)

        def copy(n, to, source):
            return remote(
                sent.at[phase, n, :, here], got.at[phase, source, :, here], (to, z), send + n, recv + source
            )

        def put(n, to, read):
            for r in range(0, rows, 8):
                sent[phase, n, :, r : r + 8, :] = own_columns(read(REACH - rows // 2 + r))

            @pl.when(t != to)
            def _():
                copy(n, to, t).start()

            @pl.when(t == to)
            def _():
                got[phase, t, :, here, :] = sent[phase, n, :, here, :]

        def take():
            @pl.when(t > 1)
            def _():
                for k in range(1, SLICES):
                    copy(2, 2, slot_of(k)).wait_recv()

        def done(pairs):
            for n, to in pairs:
                @pl.when(t != to)
                def _():
                    copy(n, to, t).wait_send()

        return put, take, done

    plain = lambda row, count: 0.0
    put_0, take_0, done_0 = deliverer(0, 16)
    for n in range(8):
        coarse_step(-(-(44 - 4 * n) // 8), w_in, w_out, win, old.at[n], plain if n < 7 else None, *scratch)
        if n < 6:
            put_0(n + 1, n + 2, rows_of(win))
        if n == FIRST_PART or n == SECOND_PART:
            part = int(n == SECOND_PART)
            recv_all(across[part])
            start_all(helped[part])
            start_all(shared[0][part])
        if n >= 6:
            recv_all(helped[n - 6])
            start_all(shared[1][n - 6])

    take_0()

    @pl.when(t > 1)
    def _():
        coarse_in_chunks(got.at[0], coarse)
        spread_coarse(coarse, lambda c, r: None, state)

    for copies in shared:
        for part in range(2):
            recv_all(copies[part])
    coefficients(
        fields.at[0], fields.at[1], pcoef, qcoef, force, (8, 16, 24, 48, 56, 64), (8, 16, 56, 64)
    )

    @pl.when(t == 1)
    def _():
        recv_all(early)
        sent_all(early)

    @pl.when(t > 0)
    def _():
        ghosts(state)
        fine_run(state, one, two, pcoef, qcoef, force)

    def sharer(phase, shift, wanted, wanted_two):
        place = lax.rem(t + shift, SLICES)
        middle = slice(16, 24)
        send, recv, around = reserve(SLICES), reserve(SLICES), reserve(4 * SLICES)

        def copy(k, slot):
            return remote(
                rolled.at[phase + 1, pl.ds(2 * slot_of(k), 3)], means.at[phase, slot, :, middle],
                (slot_of(k), z), send + k, recv + slot,
            )

        def spread(n):
            return [
                remote(
                    means.at[phase, n, :, middle], means.at[phase, n, :, 16 - 8 * d : 24 - 8 * d],
                    (t, slab_of(d)), around + 4 * n + j, around + 4 * n + j,
                )
                for j, d in enumerate((-1, 1, -2, 2))
                if abs(d) == 1 or n in wanted_two
            ]

        has_slice = functools.reduce(jnp.logical_or, [place == n for n in wanted])

        def go():
            @pl.when(has_slice)
            def _():
                spaced_tiles(block_means(state), rolled.at[phase + 1])
                for k in range(1, SLICES):
                    copy(k, place).start()
                means[phase, place, :, middle, :] = rolled[phase + 1, pl.ds(2 * t, 3)]

        def pass_on():
            for n in wanted:
                @pl.when(place != n)
                def _():
                    copy(1, n).wait_recv()

                start_all(spread(n))

        def take(n):
            recv_all(spread(n))

        def done():
            @pl.when(has_slice)
            def _():
                for k in range(1, SLICES):
                    copy(k, place).wait_send()

            for n in wanted:
                sent_all(spread(n))

        return go, pass_on, take, done

    go_1, pass_1, arrived_1, shared_1 = sharer(0, SLICES - 1, range(0, 7), range(0, 4))
    go_1()
    copy_f = remote(state.at[inside, slice(OWN, OWN + INNER)], one.at[inside, slice(OWN, OWN + INNER)], (0, z))

    @pl.when(t == 1)
    def _():
        copy_f.start()

    bulk = [
        remote(state.at[1 + a : 1 + b, rows], edge.at[side, a:b], (t, slab_of(1 - 2 * side)))
        for a, b in ((0, AHEAD), (AHEAD, CHUNK))
        for side, rows in enumerate((last_rows, first_rows))
    ]

    @pl.when(t > 0)
    def _():
        start_all(bulk[:2])

    pass_1()

    @pl.when(t > 0)
    def _():
        start_all(bulk[2:])

    def corrected(phase, n, before):
        def extra(row, count):
            there = pl.ds(row - 8, 8, stride=count)
            return means[phase, n, :, there, :] - before[n, :, pl.ds(row, 8, stride=count), :]

        return extra

    put_1, take_1, done_1 = deliverer(1, 16)
    arrived_1(0)
    win[:, 8:48, :] = means[0, 0]
    for n in range(1, 8):
        if n < 7:
            arrived_1(n)
        coarse_step(
            -(-(44 - 4 * n) // 8), w_in, w_out, win, new.at[n], corrected(0, n, old) if n < 7 else None, *scratch
        )
        if n < 7:
            put_1(n, n + 1, change(new.at[n], old.at[n]))

    take_1()

    @pl.when(t == 1)
    def _():
        copy_f.wait_send()
        got[1] = jnp.zeros(got.shape[1:], F32)

    @pl.when(t > 0)
    def _():
        recv_all(bulk)
        sent_all(bulk)
        coarse_in_chunks(got.at[1], coarse)

        def base(c, r):
            if r < 2:
                return edge[0, c, 8 * r : 8 * r + 8, :]
            if r >= 6:
                return edge[1, c, 8 * (r - 6) : 8 * (r - 6) + 8, :]
            return state[pl.ds(c.start + 1, 4), PAD + 8 * r : PAD + 8 * r + 8, :]

        spread_coarse(coarse, base, state)
        ghosts(state)
        fine_run(state, one, two, pcoef, qcoef, force)

    go_2, pass_2, arrived_2, shared_2 = sharer(1, 0, range(1, 7), range(1, 3))
    go_2()
    pass_2()

    @pl.when(t == 0)
    def _():
        copy_f.wait_recv()
        load_own(one, lam)

    @pl.when(t > 0)
    def _():
        load_own(state, lam)

    put_2, take_2, done_2 = deliverer(2, 8)
    arrived_2(1)
    win[:, 8:48, :] = means[1, 1]
    for n in range(2, 8):
        if n < 7:
            arrived_2(n)
        coarse_step(
            -(-(40 - 4 * n) // 8), w_in, w_out, win, old.at[n], corrected(1, n, new) if n < 7 else None, *scratch
        )
        put_2(n, n, change(old.at[n], new.at[n]))

    chunks_to_rows(lam, nat)
    for c in range(64):
        inputs[0, :, c * LANES : (c + 1) * LANES] = nat[c * PITCH : c * PITCH + INNER, :]
    store = pltpu.make_async_copy(inputs.at[0], out, in_sem.at[0])
    store.start()

    @pl.when(t <= 1)
    def _():
        got[2] = jnp.zeros(got.shape[1:], F32)

    sent_all(near)
    for part in range(2):
        sent_all(across[part])
        sent_all(helped[part])
        sent_all(shared[0][part])
        sent_all(shared[1][part])
    done_0([(n, n + 1) for n in range(1, 7)])
    done_1([(n, n + 1) for n in range(1, 7)])
    done_2([(n, n) for n in range(2, 8)])
    shared_1()
    shared_2()
    take_2()
    for m in range(BLOCKS):
        delta_out[m * 8 : m * 8 + 8, :] = got[2, m // 2, m % 2, 0:8, :]
    store.wait()


def finish_kernel(fine, delta, out):
    copies = jnp.where(
        lax.broadcasted_iota(jnp.int32, (LANES, 4 * LANES), 0)
        == lax.broadcasted_iota(jnp.int32, (LANES, 4 * LANES), 1) // 4, 1.0, 0.0,
    ).astype(F32)
    wide = jnp.dot(delta[...], copies, precision=HIGH, preferred_element_type=F32)
    upper = lax.broadcasted_iota(jnp.int32, (8, 4 * LANES), 0) < 4
    for m in range(delta.shape[0] // 8):
        cols = slice(m * 4 * LANES, (m + 1) * 4 * LANES)
        for a in range(INNER // 8):
            r = m * 8 + 2 * a
            v = jnp.where(upper, wide[r : r + 1], wide[r + 1 : r + 2])
            out[0, a * 8 : a * 8 + 8, cols] = fine[a * 8 : a * 8 + 8, cols] + v


def body(vorticity, stream, forcing, conv_in, conv_out):
    rows, cols = vorticity.shape
    whole = (CHUNK + 2, TALL, LANES)
    vmem = pl.BlockSpec(memory_space=VMEM)
    anywhere = pl.BlockSpec(memory_space=pl.ANY)
    window = (3, WINDOW, LANES)
    shapes = [
        (3, rows, cols), (64 * PITCH, LANES), (CHUNK * PITCH, LANES), (2,) + whole, whole, whole, whole, whole, whole,
        (4,) + whole, window, window, (SLICES,) + window, (SLICES,) + window,
        (9, 18, 8, LANES), (9, 18, 8, LANES), (3, 8, 3, 8, LANES), (8, 9, 8, LANES), (8, 9, 8, LANES),
        (3, BLOCKS + 2, 8, LANES), (2, SLICES, 3, 40, LANES), (3, SLICES, 2, 16, LANES), (3, SLICES, 2, 16, LANES),
        (2, CHUNK, HALO, LANES), (BLOCKS, 16, LANES), (8 * BLOCKS, 4 * LANES),
    ]
    slots = 176
    fine, delta = pl.pallas_call(
        kernel,
        name="parareal",
        out_shape=(jax.ShapeDtypeStruct((rows, cols), F32), jax.ShapeDtypeStruct((8 * BLOCKS, LANES), F32)),
        in_specs=[vmem, vmem, anywhere, anywhere, anywhere],
        out_specs=(anywhere, vmem),
        scratch_shapes=[VMEM(s, F32) for s in shapes]
        + [pltpu.SemaphoreType.DMA((3,)), pltpu.SemaphoreType.DMA((slots,)), pltpu.SemaphoreType.DMA((slots,))],
        compiler_params=pltpu.CompilerParams(vmem_limit_bytes=62 * 2**20, collective_id=0, has_side_effects=True),
    )(jnp.transpose(conv_in, (1, 2, 0)), jnp.transpose(conv_out, (1, 2, 0)), vorticity, stream, forcing)
    grid = 2
    return pl.pallas_call(
        finish_kernel,
        name="finish",
        grid=(grid,),
        out_shape=jax.ShapeDtypeStruct((1, rows, cols), F32),
        in_specs=[
            pl.BlockSpec((rows, cols // grid), lambda i: (0, i)),
            pl.BlockSpec((8 * BLOCKS // grid, LANES), lambda i: (i, 0)),
        ],
        out_specs=pl.BlockSpec((1, rows, cols // grid), lambda i: (0, 0, i)),
    )(fine, delta)


def solution(mesh):
    placed = (P("space", None), P("space", None), P("space", None), P(), P())
    return jax.shard_map(
        body, mesh=mesh, in_specs=placed, out_specs=P("tm", "space", None), check_vma=False
    )
```
